32 devices in a mesh: sub: 8 (over y, x, core), freq: 4 (over z).
Axes of the slice: x: 2, y: 2, z: 4, core: 2. Of those that a mesh axis runs over, the one named last changes fastest.
Arguments:
- load: float32 [8, 4, 1536, 512], P('sub', 'freq')
- a_tile: bfloat16 [8, 4, 2, 1536, 1536], P('sub', 'freq')
- left_tile: bfloat16 [8, 4, 2, 1536, 512], P('sub', 'freq'), may hold values from -0.109375 to 0.109375
- right_tile: bfloat16 [8, 4, 2, 1536, 512], P('sub', 'freq'), may hold values from -0.109375 to 0.109375
- block_mask: int32 [8, 12, 12], P('sub'), may hold values 0 or 1
- left_blocks: int32 [8, 4], P('sub'), may hold values from 0 to 11, as said below
- right_blocks: int32 [8, 4], P('sub'), may hold values from 0 to 11, as said below
- motion: float32 [4, 512], P('freq'), may hold values from -0.375 to 0.375
- freq_values: float32 [4], replicated, may hold values from 1 to 20
- node_dof: int32 [8, 512], P('sub'), may hold values from 0 to 1535
- node_owner: int32 [8, 512], P('sub'), may hold values from 0 to 3, as said below
Outputs:
- solution: float32 [8, 4, 1536, 512], P('sub', 'freq')
- spectra: float32 [8, 512, 1024], P('sub', 'freq')
The draws below stay inside these ranges and needn't reach their ends.
Inputs may be any that keep to these rules, and one draw needn't show every extreme that they name: `left_blocks`: the 4 entries of a row are distinct. `right_blocks`: the 4 entries of a row are distinct. `node_owner`: each value names exactly 128 nodes of every subdomain.
All inputs are finite; a program needn't handle non-finite values. No bound on the sum of `block_mask` on one device may be relied on, other than what follows from the above.
Results may differ from the reference program's by a relative error of at most 0.0003.
The reference program's roundings to bfloat16 on the way (of `own_tile` and `resid_bf`) count: a program that leaves them out, or rounds other values in their place, can miss the bound.
Values may be sent and summed in bfloat16 or wider, within the bound.
No kernel may reach another device: no remote copies, remote signals or barrier semaphores. Data moves between devices by JAX's collectives and lax.ppermute only.
A program may use at most 128 MiB of HBM per device.

```python
import math
import jax
import jax.numpy as jnp
from jax import lax

BS = 128
NB = 12
KB = 4
M = 1536
R = 256
F = 4
NSUB = 8
NODE_OWN = 128
NODE_SUB = 512
NOSC = 1024
NT = 64
ITERS = 2


def draw_a_tile(key, part):
    key = jax.random.fold_in(key, 11)
    full_shape = (NSUB, F, 2, NB * BS, NB * BS)
    identity = (lax.broadcasted_iota(jnp.int32, full_shape, 3) == lax.broadcasted_iota(jnp.int32, full_shape, 4)).astype(jnp.float32)
    real_index = (lax.broadcasted_iota(jnp.int32, full_shape, 2) == 0).astype(jnp.float32)
    spread = 0.5 / math.sqrt(NB * BS)
    noise_part = jax.random.normal(key, full_shape, jnp.float32)
    diagonal_value = 3.0
    return (noise_part * spread + identity * real_index * diagonal_value).astype(jnp.bfloat16)


def draw_load(key, part):
    key = jax.random.fold_in(key, 21)
    full_shape = (NSUB, F, NB * BS, 2 * R)
    position = lax.broadcasted_iota(jnp.int32, full_shape, 0).astype(jnp.float32)
    growth = 1.0 + 2.0 * position / max(NSUB - 1, 1)
    noise_part = jax.random.normal(key, full_shape, jnp.float32)
    return noise_part * growth


def distinct_blocks(key):
    scores = jax.random.randint(key, (NSUB, NB), 0, 1 << 20, dtype=jnp.int32)
    scores = scores * NB + lax.broadcasted_iota(jnp.int32, (NSUB, NB), 1)
    picked = lax.top_k(scores, KB)[1]
    return picked.astype(jnp.int32)


def draw_left_blocks(key, part):
    key = jax.random.fold_in(key, 31)
    return distinct_blocks(key)


def draw_right_blocks(key, part):
    key = jax.random.fold_in(key, 41)
    return distinct_blocks(key)


def draw_node_owner(key, part):
    key = jax.random.fold_in(key, 51)
    base_rows = lax.broadcasted_iota(jnp.int32, (NSUB, NODE_SUB), 1) // NODE_OWN
    return jax.random.permutation(key, base_rows, axis=1, independent=True).astype(jnp.int32)


def place_ends(result, key, smallest, high):
    longest = result.shape.index(max(result.shape))
    spots = []
    for shift in (0, 1):
        where = [jax.random.randint(jax.random.fold_in(key, axis), (), 0, length) for axis, length in enumerate(result.shape)]
        where[longest] = (where[longest] + shift) % result.shape[longest]
        spots.append(tuple(where))
    return result.at[spots[0]].set(smallest).at[spots[1]].set(high)


def steps_of(rng, dims, shards, smallest, high):
    loudness, own = 1.0, jax.random.fold_in(rng, 6)
    for axis_at, shards_of in shards:
        heights = jnp.exp(jax.random.uniform(jax.random.fold_in(own, axis_at), (shards_of,), jnp.float32, smallest / len(shards), high / len(shards)))
        loudness = loudness * jnp.repeat(heights, dims[axis_at] // shards_of).reshape([-1 if axis == axis_at else 1 for axis in range(len(dims))])
    return loudness


def gaussian(rng, extent, scale, limit, pieces=(), kind=jnp.bfloat16):
    result = jax.random.normal(rng, extent, jnp.float32) * scale
    if len(pieces) > 0:
        result = steps_of(rng, extent, pieces, -0.22, 0.18) * result
    return jnp.clip(result, min=-limit, max=limit).astype(kind)


def setup_inputs(seed: int = 0) -> dict:
    splits = jax.random.split(jax.random.key(seed), 12)
    load = draw_load(jax.random.fold_in(splits[11], 71), 0)
    a_tile = draw_a_tile(jax.random.fold_in(splits[11], 71), 0)
    left_tile = gaussian(splits[2], (NSUB, F, 2, M, KB * BS), (6 * KB * BS) ** -0.5, 0.109375, ((0, 8), (1, 4)))
    right_tile = gaussian(splits[3], (NSUB, F, 2, M, KB * BS), (6 * KB * BS) ** -0.5, 0.109375, ((0, 8), (1, 4)))
    block_mask = place_ends((jax.random.randint(splits[4], (NSUB, NB, NB), 0, 2) < 1).astype(jnp.int32), jax.random.fold_in(splits[4], 1), 0, 1)
    left_blocks = draw_left_blocks(jax.random.fold_in(splits[11], 71), 0)
    right_blocks = draw_right_blocks(jax.random.fold_in(splits[11], 71), 0)
    motion = gaussian(splits[7], (F, 2 * R), R ** -0.5, 0.375, ((0, 4),), jnp.float32)
    freq_values = jnp.clip(jnp.exp(jax.random.uniform(splits[8], (F,), jnp.float32, math.log(1.0), math.log(20.0))), 1.0, 20.0)
    node_dof = place_ends(jax.random.randint(splits[9], (NSUB, NODE_SUB), 0, M), jax.random.fold_in(splits[9], 1), 0, M - 1).astype(jnp.int32)
    node_owner = draw_node_owner(jax.random.fold_in(splits[11], 71), 0)
    return dict(load=load, a_tile=a_tile, left_tile=left_tile, right_tile=right_tile, block_mask=block_mask, left_blocks=left_blocks, right_blocks=right_blocks, motion=motion, freq_values=freq_values, node_dof=node_dof, node_owner=node_owner)


EPSILON = 1e-6
DAMPING = 0.05
TIME_STEP = 0.01


def masked_tile(tile_pair, pattern):
    block_count = pattern.shape[0]
    block_rows = tile_pair.shape[-1] // block_count
    identity = (jnp.arange(block_count)[:, None] == jnp.arange(block_count)[None, :]).astype(jnp.int32)
    keep_blocks = jnp.maximum(pattern, identity)
    keep_full = jnp.repeat(jnp.repeat(keep_blocks, block_rows, axis=0), block_rows, axis=1)
    return tile_pair * keep_full.astype(tile_pair.dtype)[None, None]


def select_blocks(vectors, block_ids):
    count_f, row_count, col_count = vectors.shape
    blocked = vectors.reshape(count_f, NB, row_count // NB, col_count)
    picked = jnp.take(blocked, block_ids, axis=1)
    return picked.reshape(count_f, -1, col_count)


def tile_product(tile_pair, vectors):
    half_cols = vectors.shape[-1] // 2
    product = jnp.einsum('fcmk,fkr->fcmr', tile_pair.astype(jnp.float32), vectors.astype(jnp.float32), precision=lax.Precision.HIGHEST)
    real_part = product[:, 0, :, :half_cols] - product[:, 1, :, half_cols:]
    imag_part = product[:, 0, :, half_cols:] + product[:, 1, :, :half_cols]
    return jnp.concatenate([real_part, imag_part], axis=-1)


def response_table(freq_values, sample_count, osc_count):
    count_f = freq_values.shape[0]
    omega_load = 2.0 * math.pi * freq_values.astype(jnp.float32)
    omega_osc = 2.0 * math.pi * 0.5 * 100.0 ** (jnp.arange(osc_count, dtype=jnp.float32) / (osc_count - 1))
    sample_times = jnp.arange(sample_count, dtype=jnp.float32) * TIME_STEP
    stiffness = (omega_osc * omega_osc)[None, :]
    damping_term = 2.0 * DAMPING * omega_osc[None, :] * omega_load[:, None]
    detuning = stiffness - (omega_load * omega_load)[:, None]
    denominator = detuning * detuning + damping_term * damping_term
    gain_real = (stiffness * detuning + damping_term * damping_term) / denominator / count_f
    gain_imag = (damping_term * detuning - stiffness * damping_term) / denominator / count_f
    phase = omega_load[:, None] * sample_times[None, :]
    cosine = jnp.cos(phase)[:, :, None]
    sine = jnp.sin(phase)[:, :, None]
    table_real = cosine * gain_real[:, None, :] - sine * gain_imag[:, None, :]
    table_imag = sine * gain_real[:, None, :] + cosine * gain_imag[:, None, :]
    stacked = jnp.concatenate([table_real, -table_imag], axis=0)
    return stacked.reshape(2 * count_f, sample_count * osc_count)


def node_spectra(response, table, sample_count):
    node_count = response.shape[0]
    block_size = math.gcd(node_count, 32)
    blocks = response.reshape(node_count // block_size, block_size, response.shape[1])

    def one_block(block_rows):
        history = jnp.dot(block_rows, table, precision=lax.Precision.HIGHEST, preferred_element_type=jnp.float32)
        history = history.reshape(block_size, sample_count, -1)
        return jnp.max(jnp.abs(history), axis=1)

    return lax.map(one_block, blocks).reshape(node_count, -1)


def reference(load, a_tile, left_tile, right_tile, block_mask, left_blocks, right_blocks, motion, freq_values, node_dof, node_owner):
    half_cols = load.shape[-1] // 2

    def apply_operator(resid_bf):
        zero_rows = jnp.zeros_like(resid_bf[:1])
        padded = jnp.concatenate([zero_rows, resid_bf, zero_rows], axis=0)

        def one_sub(position):
            own_tile = masked_tile(a_tile[position], block_mask[position])
            below_faces = select_blocks(padded[position], left_blocks[position])
            above_faces = select_blocks(padded[position + 2], right_blocks[position])
            return (tile_product(own_tile, resid_bf[position])
                    + tile_product(left_tile[position], below_faces)
                    + tile_product(right_tile[position], above_faces))

        return lax.map(one_sub, jnp.arange(NSUB, dtype=jnp.int32))

    solution = jnp.zeros_like(load)
    residual = load
    for step in range(ITERS):
        resid_bf = residual.astype(jnp.bfloat16)
        image = apply_operator(resid_bf)
        resid_real, resid_imag = residual[..., :half_cols], residual[..., half_cols:]
        image_real, image_imag = image[..., :half_cols], image[..., half_cols:]
        cross_real = jnp.sum(image_real * resid_real + image_imag * resid_imag, axis=(0, 2))
        cross_imag = jnp.sum(image_real * resid_imag - image_imag * resid_real, axis=(0, 2))
        energy = jnp.sum(image_real * image_real + image_imag * image_imag, axis=(0, 2)) + EPSILON
        alpha_real = (cross_real / energy)[None, :, None, :]
        alpha_imag = (cross_imag / energy)[None, :, None, :]
        solution = solution + jnp.concatenate([alpha_real * resid_real - alpha_imag * resid_imag, alpha_real * resid_imag + alpha_imag * resid_real], axis=-1)
        residual = residual - jnp.concatenate([alpha_real * image_real - alpha_imag * image_imag, alpha_real * image_imag + alpha_imag * image_real], axis=-1)

    picked = jnp.take_along_axis(solution, node_dof.astype(jnp.int32)[:, None, :, None], axis=2)
    motion_real = motion[:, :half_cols][None, :, None, :]
    motion_imag = motion[:, half_cols:][None, :, None, :]
    pick_real, pick_imag = picked[..., :half_cols], picked[..., half_cols:]
    resp_real = jnp.sum(pick_real * motion_real - pick_imag * motion_imag, axis=-1)
    resp_imag = jnp.sum(pick_real * motion_imag + pick_imag * motion_real, axis=-1)
    ordering = jnp.argsort(node_owner, axis=1, stable=True).astype(jnp.int32)
    resp_real = jnp.take_along_axis(resp_real, ordering[:, None, :], axis=2)
    resp_imag = jnp.take_along_axis(resp_imag, ordering[:, None, :], axis=2)
    stacked = jnp.stack([resp_real, resp_imag], axis=1)
    response = jnp.transpose(stacked, (0, 3, 1, 2)).reshape(NSUB * NODE_SUB, 2 * F)
    table = response_table(freq_values, NT, NOSC)
    spectra = node_spectra(response, table, NT).reshape(NSUB, NODE_SUB, NOSC)
    return solution, spectra
```

```python
import functools
import math

import jax
import jax.numpy as jnp
from jax import lax
from jax.experimental import pallas as pl
from jax.experimental.pallas import tpu as pltpu
from jax.sharding import PartitionSpec as P

NB = 12
NOSC = 1024
NT = 64
KGROUP = 8
EPSILON = 1e-06
DAMPING = 0.05
TIME_STEP = 0.01
MIB = 1024 * 1024

VM = pl.BlockSpec(memory_space=pltpu.VMEM)
SM = pl.BlockSpec(memory_space=pltpu.SMEM)
HB = pl.BlockSpec(memory_space=pl.ANY)
F32 = jnp.float32
BF16 = jnp.bfloat16


def vmem(*arrays):
    return [pltpu.with_memory_space_constraint(x, pltpu.VMEM) for x in arrays]


def call(kernel, outs, in_specs, out_specs, scratch=(), flops=0, moved=0, limit=40):
    return pl.pallas_call(
        kernel,
        out_shape=outs,
        in_specs=in_specs,
        out_specs=out_specs,
        scratch_shapes=list(scratch),
        compiler_params=pltpu.CompilerParams(vmem_limit_bytes=limit * MIB),
        cost_estimate=pl.CostEstimate(flops=flops, bytes_accessed=moved, transcendentals=0),
    )


def turned(v):
    half = v.shape[-1] // 2
    return jnp.concatenate([-v[:, half:], v[:, :half]], axis=1)


def load_kernel(load_ref, v0_ref, vb_ref, sems):
    chunks = sems.shape[0]
    rows = v0_ref.shape[0] // chunks
    copies = [
        pltpu.make_async_copy(
            load_ref.at[pl.ds(c * rows, rows)], v0_ref.at[pl.ds(c * rows, rows)], sems.at[c]
        )
        for c in range(chunks)
    ]
    for copy in copies:
        copy.start()
    for c, copy in enumerate(copies):
        copy.wait()
        vb_ref[c * rows : (c + 1) * rows] = v0_ref[c * rows : (c + 1) * rows].astype(BF16)


def pack_kernel(ida_ref, idb_ref, vb_ref, sa_ref, sb_ref):
    count = ida_ref.shape[0]
    rows = sa_ref.shape[0] // count
    for b in range(count):
        to = slice(b * rows, (b + 1) * rows)
        sb_ref[to] = vb_ref[pl.ds(pl.multiple_of(idb_ref[b] * rows, rows), rows)]
    for b in range(count):
        to = slice(b * rows, (b + 1) * rows)
        sa_ref[to] = vb_ref[pl.ds(pl.multiple_of(ida_ref[b] * rows, rows), rows)]


def own_kernel(first, step, mask_ref, par_ref, a_ref, *rest):
    if first:
        l_ref, r_ref, v_ref, ra_ref, own_ref, ta_ref, tb_ref, abuf, rhs, sems, tsems = rest
    else:
        ta_ref, v_ref, ra_ref, own_ref, abuf, rhs, sems = rest
    m, face = v_ref.shape[0], ra_ref.shape[0]
    blocks = m // step
    bs = m // NB
    for i in range(blocks):
        rows = pl.ds(i * step, step)
        pltpu.make_async_copy(a_ref.at[:, rows], abuf.at[:, rows], sems.at[i]).start()
        if first:

            @pl.when(par_ref[0] == 0)
            def _():
                pltpu.make_async_copy(r_ref.at[:, rows], ta_ref.at[:, rows], tsems.at[i]).start()

            @pl.when(par_ref[0] != 0)
            def _():
                pltpu.make_async_copy(l_ref.at[:, rows], ta_ref.at[:, rows], tsems.at[i]).start()

    if first:

        @pl.when(par_ref[0] == 0)
        def _():
            pltpu.make_async_copy(l_ref, tb_ref, tsems.at[blocks]).start()

        @pl.when(par_ref[0] != 0)
        def _():
            pltpu.make_async_copy(r_ref, tb_ref, tsems.at[blocks]).start()

    v = v_ref[...]
    rhs[0:m] = v
    rhs[m : 2 * m] = turned(v)
    ra = ra_ref[...]
    rhs[2 * m : 2 * m + face] = ra
    rhs[2 * m + face :] = turned(ra)

    @pl.loop(0, blocks)
    def _(i):
        rows = pl.ds(pl.multiple_of(i * step, step), step)
        pltpu.make_async_copy(a_ref.at[:, rows], abuf.at[:, rows], sems.at[i]).wait()
        if first:
            pltpu.make_async_copy(l_ref.at[:, rows], ta_ref.at[:, rows], tsems.at[i]).wait()
        for sub in range(step // bs):
            brow = i * (step // bs) + sub
            at = pl.ds(pl.multiple_of(i * step + sub * bs, bs), bs)
            for j in range(NB):

                @pl.when((mask_ref[brow * NB + j] == 0) & (brow != j))
                def _():
                    abuf[:, at, j * bs : (j + 1) * bs] = jnp.zeros((2, bs, bs), BF16)

        lhs = jnp.concatenate(
            [abuf[0, rows, :], abuf[1, rows, :], ta_ref[0, rows, :], ta_ref[1, rows, :]], axis=1
        )
        own_ref[rows, :] = jnp.dot(lhs, rhs[...], preferred_element_type=F32)

    if first:
        pltpu.make_async_copy(l_ref, tb_ref, tsems.at[blocks]).wait()


def far_rhs(rb_ref, rhs):
    rb = rb_ref[...]
    face = rb.shape[0]
    rhs[0:face] = rb
    rhs[face:] = turned(rb)


def faces_kernel(idb_ref, own_ref, tb_ref, rb_ref, sb_ref, rhs, lhs):
    count = idb_ref.shape[0]
    face = rb_ref.shape[0]
    rows = face // count
    far_rhs(rb_ref, rhs)
    for b in range(count):
        at = pl.ds(pl.multiple_of(idb_ref[b] * rows, rows), rows)
        lhs[b * rows : (b + 1) * rows, 0:face] = tb_ref[0, at, :]
        lhs[b * rows : (b + 1) * rows, face:] = tb_ref[1, at, :]
    part = jnp.dot(lhs[...], rhs[...], preferred_element_type=F32)
    for b in range(count):
        at = pl.ds(pl.multiple_of(idb_ref[b] * rows, rows), rows)
        to = slice(b * rows, (b + 1) * rows)
        sb_ref[to] = (own_ref[at, :] + part[to]).astype(BF16)


def fold(x):
    return jnp.sum(x.reshape(x.shape[0] // 8, 8, x.shape[1]), axis=0)


def image_kernel(step, ida_ref, own_ref, tb_ref, rb_ref, v0_ref, v1_ref, vb_ref, sa_ref, s_ref, rhs):
    m = own_ref.shape[0]
    half = v0_ref.shape[1] // 2
    far_rhs(rb_ref, rhs)

    def body(i, acc):
        rows = pl.ds(pl.multiple_of(i * step, step), step)
        lhs = jnp.concatenate([tb_ref[0, rows, :], tb_ref[1, rows, :]], axis=1)
        v1 = own_ref[rows, :] + jnp.dot(lhs, rhs[...], preferred_element_type=F32)
        v1_ref[rows, :] = v1
        vb_ref[rows, :] = v1.astype(BF16)
        ar, ai = v0_ref[rows, :half], v0_ref[rows, half:]
        br, bi = v1[:, :half], v1[:, half:]
        return (
            acc[0] + fold(br * ar + bi * ai),
            acc[1] + fold(br * ai - bi * ar),
            acc[2] + fold(br * br + bi * bi),
        )

    zero = jnp.zeros((8, half), F32)
    acc = lax.fori_loop(0, m // step, body, (zero, zero, zero))
    for k in range(3):
        s_ref[k : k + 1, :] = jnp.sum(acc[k], axis=0, keepdims=True)
    s_ref[3:, :] = jnp.zeros((5, half), F32)
    count = ida_ref.shape[0]
    bs = sa_ref.shape[0] // count
    for b in range(count):
        at = pl.ds(pl.multiple_of(ida_ref[b] * bs, bs), bs)
        sa_ref[b * bs : (b + 1) * bs] = vb_ref[at]


def second_kernel(step, own_ref, tb_ref, rb_ref, v0_ref, v1_ref, s1_ref, s_ref, rhs):
    m = own_ref.shape[0]
    half = v0_ref.shape[1] // 2
    far_rhs(rb_ref, rhs)

    def body(i, acc):
        rows = pl.ds(pl.multiple_of(i * step, step), step)
        lhs = jnp.concatenate([tb_ref[0, rows, :], tb_ref[1, rows, :]], axis=1)
        w = own_ref[rows, :] + jnp.dot(lhs, rhs[...], preferred_element_type=F32)
        ar, ai = v0_ref[rows, :half], v0_ref[rows, half:]
        br, bi = v1_ref[rows, :half], v1_ref[rows, half:]
        wr, wi = w[:, :half], w[:, half:]
        return (
            acc[0] + fold(wr * ar + wi * ai),
            acc[1] + fold(wr * ai - wi * ar),
            acc[2] + fold(wr * br + wi * bi),
            acc[3] + fold(wr * bi - wi * br),
            acc[4] + fold(wr * wr + wi * wi),
        )

    zero = jnp.zeros((8, half), F32)
    acc = lax.fori_loop(0, m // step, body, (zero,) * 5)
    s_ref[...] = s1_ref[...]
    for k in range(5):
        s_ref[3 + k : 4 + k, :] = jnp.sum(acc[k], axis=0, keepdims=True)


def pick_kernel(dof_ref, v0_ref, v1_ref, out_ref):
    cols = v0_ref.shape[1]

    @pl.loop(0, out_ref.shape[0] // 8)
    def _(g):
        base = pl.multiple_of(g * 8, 8)
        at = [dof_ref[base + r] for r in range(8)]
        out_ref[pl.ds(base, 8), :cols] = jnp.concatenate(
            [v0_ref[pl.ds(a, 1), :] for a in at], axis=0
        )
        out_ref[pl.ds(base, 8), cols:] = jnp.concatenate(
            [v1_ref[pl.ds(a, 1), :] for a in at], axis=0
        )


def cmul(x, y):
    return x[0] * y[0] - x[1] * y[1], x[0] * y[1] + x[1] * y[0]


def resp_kernel(s_ref, motion_ref, pick_ref, r_ref, h_ref):
    half = s_ref.shape[1]
    row = lambda k: s_ref[k : k + 1, :]
    cross1, energy1 = (row(0), row(1)), row(2)
    a1 = tuple(c / (energy1 + EPSILON) for c in cross1)
    conj = (a1[0], -a1[1])
    wv0, wv1, ww = (row(3), row(4)), (row(5), row(6)), row(7)
    size = a1[0] * a1[0] + a1[1] * a1[1]
    p0, p1 = cmul(conj, wv0), cmul(conj, wv1)
    cross2 = tuple(a1[k] * EPSILON - p0[k] + size * wv1[k] for k in range(2))
    energy2 = jnp.maximum(energy1 - 2.0 * p1[0] + size * ww, 0.0)
    a2 = tuple(c / (energy2 + EPSILON) for c in cross2)
    both = cmul(a1, a2)
    h0 = (a1[0] + a2[0], a1[1] + a2[1])
    h1 = (-both[0], -both[1])
    h_ref[0:1], h_ref[1:2], h_ref[2:3], h_ref[3:4] = h0[0], h0[1], h1[0], h1[1]
    h_ref[4:] = jnp.zeros((4, half), F32)
    mo = (motion_ref[0:1, :half], motion_ref[0:1, half:])
    g0, g1 = cmul(h0, mo), cmul(h1, mo)
    chunk = 128
    for i in range(pick_ref.shape[0] // chunk):
        rows = slice(i * chunk, (i + 1) * chunk)
        re = im = None
        for t in range(half // 128):
            at = slice(t * 128, (t + 1) * 128)
            x = [pick_ref[rows, k * half + t * 128 : k * half + (t + 1) * 128] for k in range(4)]
            c = [g[:, at] for g in (*g0, *g1)]
            one = c[0] * x[0] - c[1] * x[1] + c[2] * x[2] - c[3] * x[3]
            two = c[0] * x[1] + c[1] * x[0] + c[2] * x[3] + c[3] * x[2]
            re = one if re is None else re + one
            im = two if im is None else im + two
        r_ref[0:1, rows] = jnp.sum(re.T, axis=0, keepdims=True)
        r_ref[1:2, rows] = jnp.sum(im.T, axis=0, keepdims=True)


def sol_kernel(h_ref, v0_ref, v1_ref, out_ref, buf, sems):
    chunks = sems.shape[0]
    half = h_ref.shape[1]
    rows = buf.shape[0] // chunks
    h = [h_ref[k : k + 1, :] for k in range(4)]
    for c in range(chunks):
        at = slice(c * rows, (c + 1) * rows)
        ar, ai = v0_ref[at, :half], v0_ref[at, half:]
        br, bi = v1_ref[at, :half], v1_ref[at, half:]
        buf[at, :half] = h[0] * ar - h[1] * ai + h[2] * br - h[3] * bi
        buf[at, half:] = h[0] * ai + h[1] * ar + h[2] * bi + h[3] * br
        pltpu.make_async_copy(
            buf.at[pl.ds(c * rows, rows)], out_ref.at[pl.ds(c * rows, rows)], sems.at[c]
        ).start()
    for c in range(chunks):
        pltpu.make_async_copy(
            buf.at[pl.ds(c * rows, rows)], out_ref.at[pl.ds(c * rows, rows)], sems.at[c]
        ).wait()


def table_kernel(fcount, wl_ref, x_ref, y_ref, out_ref):
    groups, nosc, lanes = out_ref.shape
    step = 128
    wl = wl_ref[0:1, :]
    low = (lax.broadcasted_iota(jnp.int32, (step, lanes), 1) // (2 * fcount)) % 4 >= 2

    @pl.loop(0, nosc // step)
    def _(b):
        rows = pl.ds(pl.multiple_of(b * step, step), step)
        index = (lax.broadcasted_iota(jnp.int32, (step, lanes), 0) + b * step).astype(F32)
        osc = (2.0 * math.pi * 0.5) * jnp.exp(index * (math.log(100.0) / (nosc - 1)))
        stiffness = osc * osc
        damping = 2.0 * DAMPING * osc * wl
        detuning = stiffness - wl * wl
        scale = 1.0 / ((detuning * detuning + damping * damping) * fcount)
        gr = (stiffness * detuning + damping * damping) * scale
        gi = (damping * detuning - stiffness * damping) * scale
        for k in range(groups):
            value = x_ref[k : k + 1, :] * gr + y_ref[k : k + 1, :] * gi
            high = value.astype(BF16).astype(F32)
            out_ref[k, rows, :] = jnp.where(low, value - high, high).astype(BF16)


def spec_kernel(step, me_ref, *rest):
    r_refs, (t_ref, out_ref, rhs) = rest[:-3], rest[-3:]
    groups, nosc, lanes = t_ref.shape
    nodes = out_ref.shape[0]
    per = lanes // KGROUP
    at = pl.ds(pl.multiple_of(me_ref[0] * nodes, nodes), nodes)
    r = jnp.concatenate([ref[:, at] for ref in r_refs], axis=0)
    high = r.astype(BF16).astype(F32)
    parts = jnp.concatenate([high, r - high, high, r - high], axis=0).astype(BF16)
    rhs[...] = jnp.zeros(rhs.shape, BF16)
    for k in range(KGROUP):
        rhs[k * per : (k + 1) * per, k * nodes : (k + 1) * nodes] = parts

    @pl.loop(0, nosc // step)
    def _(b):
        rows = pl.ds(pl.multiple_of(b * step, step), step)
        best = None
        for g in range(groups):
            history = jnp.dot(t_ref[g, rows, :], rhs[...], preferred_element_type=F32)
            for k in range(KGROUP):
                one = jnp.abs(history[:, k * nodes : (k + 1) * nodes])
                best = one if best is None else jnp.maximum(best, one)
        out_ref[:, rows] = best.T


def exchange(x, axis, count, bit):
    return lax.ppermute(x, axis, [(i, i ^ bit) for i in range(count)])


def total(x, axis):
    count = lax.axis_size(axis)
    if count & (count - 1):
        return lax.psum(x, axis)
    bit = 1
    while bit < count:
        x = x + exchange(x, axis, count, bit)
        bit *= 2
    return x


def everyone(x, axis):
    count = lax.axis_size(axis)
    bit = 1
    parts = x
    while bit < count:
        parts = jnp.concatenate([parts, exchange(parts, axis, count, bit)], axis=0)
        bit *= 2
    return parts


def on_device(
    load,
    a_tile,
    left_tile,
    right_tile,
    block_mask,
    left_blocks,
    right_blocks,
    motion,
    freq_values,
    node_dof,
    node_owner,
):
    m, cols = load.shape[2:]
    half = cols // 2
    face = left_tile.shape[-1]
    bs = m // NB
    nsub, fcount = lax.axis_size("sub"), lax.axis_size("freq")
    sub, freq = lax.axis_index("sub"), lax.axis_index("freq")
    nodes_sub = node_dof.shape[1]
    nodes_own = nodes_sub // fcount
    parity = (sub % 2).astype(jnp.int32)
    even = parity == 0

    def swap_pairs(x, start):
        pairs = []
        for i in range(start, nsub - 1, 2):
            pairs += [(i, i + 1), (i + 1, i)]
        return lax.ppermute(x, "sub", pairs)

    near = functools.partial(swap_pairs, start=0)
    far = functools.partial(swap_pairs, start=1)

    left_ids, right_ids = left_blocks[0], right_blocks[0]
    send_b = far(jnp.where(even, left_ids, right_ids))
    send_a = near(jnp.where(even, right_ids, left_ids))

    v0, vb = call(
        load_kernel,
        (pltpu.VMEM((m, cols), F32), pltpu.VMEM((m, cols), BF16)),
        [HB],
        (VM, VM),
        [pltpu.SemaphoreType.DMA((4,))],
        moved=2 * m * cols * 4,
    )(load[0, 0])

    packed = jax.ShapeDtypeStruct((face, cols), BF16)
    pack_a, pack_b = call(pack_kernel, (packed, packed), [SM, SM, VM], (VM, VM), moved=m * cols * 2)(
        send_a, send_b, *vmem(vb)
    )
    far1, near1 = far(pack_b), near(pack_a)

    mask = block_mask[0].reshape(-1)
    parity1 = parity.reshape(1)
    step = 512
    own_scratch = [
        pltpu.VMEM((2, m, m), BF16),
        pltpu.VMEM((2 * m + 2 * face, cols), BF16),
        pltpu.SemaphoreType.DMA((m // step,)),
    ]
    own_flops = 2 * m * (2 * m + 2 * face) * cols
    own1, tile_a, tile_b = call(
        functools.partial(own_kernel, True, step),
        (
            pltpu.VMEM((m, cols), F32),
            pltpu.VMEM((2, m, face), BF16),
            pltpu.VMEM((2, m, face), BF16),
        ),
        [SM, SM, HB, HB, HB, VM, VM],
        (VM, VM, VM),
        own_scratch + [pltpu.SemaphoreType.DMA((m // step + 1,))],
        flops=own_flops,
        moved=4 * m * (m + 2 * face),
    )(mask, parity1, a_tile[0, 0], left_tile[0, 0], right_tile[0, 0], *vmem(vb), near1)

    rhs_scratch = pltpu.VMEM((2 * face, cols), BF16)
    pack_b2 = call(
        faces_kernel,
        packed,
        [SM, VM, VM, VM],
        VM,
        [rhs_scratch, pltpu.VMEM((face, 2 * face), BF16)],
        flops=4 * face * face * cols,
    )(send_b, *vmem(own1, tile_b), far1)
    far2 = far(pack_b2)

    v1, v1b, pack_a2, sums1 = call(
        functools.partial(image_kernel, 256),
        (
            pltpu.VMEM((m, cols), F32),
            pltpu.VMEM((m, cols), BF16),
            packed,
            jax.ShapeDtypeStruct((8, half), F32),
        ),
        [SM, VM, VM, VM, VM],
        (VM, VM, VM, VM),
        [rhs_scratch],
        flops=4 * m * face * cols,
    )(send_a, *vmem(own1, tile_b), far1, *vmem(v0))
    near2 = near(pack_a2)

    own2 = call(
        functools.partial(own_kernel, False, step),
        pltpu.VMEM((m, cols), F32),
        [SM, SM, HB, VM, VM, VM],
        VM,
        own_scratch,
        flops=own_flops,
        moved=4 * m * (m + face),
    )(mask, parity1, a_tile[0, 0], *vmem(tile_a, v1b), near2)

    owner, dof = node_owner[0], node_dof[0]
    number = jnp.arange(nodes_sub, dtype=jnp.int32)
    before = (owner[:, None] == owner[None, :]) & (number[None, :] < number[:, None])
    slot = owner * nodes_own + jnp.sum(before.astype(jnp.int32), axis=1)
    dof_of = jnp.sum(jnp.where(slot[None, :] == number[:, None], dof[None, :], 0), axis=1)
    picks = call(
        pick_kernel,
        pltpu.VMEM((nodes_sub, 2 * cols), F32),
        [SM, VM, VM],
        VM,
        moved=nodes_sub * cols * 16,
    )(dof_of, *vmem(v0, v1))

    lanes = KGROUP * 8 * fcount
    lane = jnp.arange(lanes, dtype=jnp.int32)
    of = (lane % (2 * fcount)) // 2
    wl = jnp.zeros((lanes,), F32)
    for p in range(fcount):
        wl = jnp.where(of == p, 2.0 * math.pi * freq_values[freq ^ p], wl)
    times = (
        jnp.arange(NT // KGROUP, dtype=jnp.int32)[:, None] * KGROUP + lane[None, :] // (8 * fcount)
    ).astype(F32) * TIME_STEP
    phase = wl[None, :] * times
    cosine, sine = jnp.cos(phase), jnp.sin(phase)
    real = (lane % 2 == 0)[None, :]
    table = call(
        functools.partial(table_kernel, fcount),
        pltpu.VMEM((NT // KGROUP, NOSC, lanes), BF16),
        [VM, VM, VM],
        VM,
        moved=NT * NOSC * 16,
    )(wl[None, :], jnp.where(real, cosine, -sine), jnp.where(real, -sine, -cosine))

    sums = call(
        functools.partial(second_kernel, 256),
        jax.ShapeDtypeStruct((8, half), F32),
        [VM] * 6,
        VM,
        [rhs_scratch],
        flops=4 * m * face * cols,
    )(*vmem(own2, tile_b), far2, *vmem(v0, v1), sums1)
    sums = total(sums, "sub")

    resp, h = call(
        resp_kernel,
        (jax.ShapeDtypeStruct((2, nodes_sub), F32), jax.ShapeDtypeStruct((8, half), F32)),
        [VM, VM, VM],
        (VM, VM),
    )(sums, motion, *vmem(picks))
    arrived = everyone(resp, "freq")
    solution = call(
        sol_kernel,
        jax.ShapeDtypeStruct((m, cols), F32),
        [VM, VM, VM],
        HB,
        [pltpu.VMEM((m, cols), F32), pltpu.SemaphoreType.DMA((6,))],
        moved=m * cols * 12,
    )(h, *vmem(v0, v1))

    spectra = call(
        functools.partial(spec_kernel, 128),
        jax.ShapeDtypeStruct((nodes_own, NOSC), F32),
        [SM, VM, VM],
        VM,
        [pltpu.VMEM((lanes, KGROUP * nodes_own), BF16)],
        flops=2 * NOSC * (NT // KGROUP) * lanes * KGROUP * nodes_own,
    )(freq.astype(jnp.int32).reshape(1), arrived, *vmem(table))
    return solution[None, None], spectra[None]


def solution(mesh):
    placed = (
        P("sub", "freq", None, None),
        P("sub", "freq", None, None, None),
        P("sub", "freq", None, None, None),
        P("sub", "freq", None, None, None),
        P("sub", None, None),
        P("sub", None),
        P("sub", None),
        P("freq", None),
        P(),
        P("sub", None),
        P("sub", None),
    )
    return jax.shard_map(
        on_device,
        mesh=mesh,
        in_specs=placed,
        out_specs=(P("sub", "freq", None, None), P("sub", "freq", None)),
        check_vma=False,
    )
```

```python
import functools
import math

import jax
import jax.numpy as jnp
from jax import lax
from jax.experimental import pallas as pl
from jax.experimental.pallas import tpu as pltpu
from jax.sharding import PartitionSpec as P

NB = 12
NOSC = 1024
NT = 64
KGROUP = 8
EPSILON = 1e-06
DAMPING = 0.05
TIME_STEP = 0.01
MIB = 1024 * 1024

VM = pl.BlockSpec(memory_space=pltpu.VMEM)
SM = pl.BlockSpec(memory_space=pltpu.SMEM)
HB = pl.BlockSpec(memory_space=pl.ANY)
F32 = jnp.float32
BF16 = jnp.bfloat16


def hbm(*arrays):
    return [pltpu.with_memory_space_constraint(x, pltpu.HBM) for x in arrays]


def vmem(*arrays):
    return [pltpu.with_memory_space_constraint(x, pltpu.VMEM) for x in arrays]


def call(kernel, outs, in_specs, out_specs, scratch=(), limit=40):
    return pl.pallas_call(
        kernel,
        out_shape=outs,
        in_specs=in_specs,
        out_specs=out_specs,
        scratch_shapes=list(scratch),
        compiler_params=pltpu.CompilerParams(vmem_limit_bytes=limit * MIB),
    )


def turned(v):
    half = v.shape[-1] // 2
    return jnp.concatenate([-v[:, half:], v[:, :half]], axis=1)


def pack_kernel(ida_ref, idb_ref, load_ref, sa_ref, sb_ref, buf, sems):
    count = ida_ref.shape[0]
    rows = sa_ref.shape[0] // count
    lists = ((idb_ref, sb_ref), (ida_ref, sa_ref))

    def fetch(k, b):
        at = pl.ds(pl.multiple_of(lists[k][0][b] * rows, rows), rows)
        return pltpu.make_async_copy(load_ref.at[at], buf.at[k, b], sems.at[k, b])

    for k in range(2):
        for b in range(count):
            fetch(k, b).start()
    for k in range(2):
        for b in range(count):
            fetch(k, b).wait()
            lists[k][1][b * rows : (b + 1) * rows] = buf[k, b].astype(BF16)


def own_kernel(first, step, mask_ref, par_ref, a_ref, *rest):
    if first:
        lh_ref, rh_ref, v_ref, ra_ref, _, own_ref, l_ref, r_ref, rhs, sems = rest
    else:
        l_ref, r_ref, v_ref, ra_ref, _, own_ref, rhs = rest
    m, face = v_ref.shape[0], ra_ref.shape[0]
    bs = m // NB

    def fetch(i, k):
        rows = pl.ds(pl.multiple_of(i * step, step), step)
        source, to = ((lh_ref, l_ref), (rh_ref, r_ref))[k]
        return pltpu.make_async_copy(source.at[:, rows], to.at[:, rows], sems.at[i, k])

    if first:
        for i in range(m // step):
            for k in range(2):
                fetch(i, k).start()
    v = v_ref[...].astype(BF16)
    rhs[0:m] = v
    rhs[m : 2 * m] = turned(v)
    ra = ra_ref[...]
    rhs[2 * m : 2 * m + face] = ra
    rhs[2 * m + face :] = turned(ra)
    even = par_ref[0] == 0

    @pl.loop(0, m // step)
    def _(i):
        if first:
            fetch(i, 0).wait()
            fetch(i, 1).wait()
        lhs = []
        for sub in range(step // bs):
            brow = i * (step // bs) + sub
            at = pl.ds(pl.multiple_of(i * step + sub * bs, bs), bs)
            keep = [(mask_ref[brow, j] != 0) | (brow == j) for j in range(NB)]
            pieces = []
            for c in range(2):
                for j in range(NB):
                    block = a_ref[c, at, j * bs : (j + 1) * bs]
                    pieces.append(lax.select(keep[j], block, jnp.zeros_like(block)))
            for c in range(2):
                pieces.append(lax.select(even, r_ref[c, at, :], l_ref[c, at, :]))
            lhs.append(jnp.concatenate(pieces, axis=1))
        rows = pl.ds(pl.multiple_of(i * step, step), step)
        own_ref[rows, :] = jnp.dot(
            jnp.concatenate(lhs, axis=0), rhs[...], preferred_element_type=F32
        )


def far_rhs(rb_ref, rhs):
    rb = rb_ref[...]
    face = rb.shape[0]
    rhs[0:face] = rb
    rhs[face:] = turned(rb)


def far_lhs(par_ref, l_ref, r_ref, rows):
    even = par_ref[0] == 0
    return jnp.concatenate(
        [lax.select(even, l_ref[c, rows, :], r_ref[c, rows, :]) for c in range(2)], axis=1
    )


def faces_kernel(idb_ref, par_ref, own_ref, l_ref, r_ref, rb_ref, sb_ref, rhs, lhs):
    count = idb_ref.shape[0]
    face = rb_ref.shape[0]
    rows = face // count
    far_rhs(rb_ref, rhs)
    for b in range(count):
        at = pl.ds(pl.multiple_of(idb_ref[b] * rows, rows), rows)
        lhs[b * rows : (b + 1) * rows] = far_lhs(par_ref, l_ref, r_ref, at)
    part = jnp.dot(lhs[...], rhs[...], preferred_element_type=F32)
    for b in range(count):
        at = pl.ds(pl.multiple_of(idb_ref[b] * rows, rows), rows)
        to = slice(b * rows, (b + 1) * rows)
        sb_ref[to] = (own_ref[at, :] + part[to]).astype(BF16)


def fold(x):
    return jnp.sum(x.reshape(x.shape[0] // 8, 8, x.shape[1]), axis=0)


def image_kernel(step, ida_ref, par_ref, own_ref, l_ref, r_ref, rb_ref, v0_ref, after, *rest):
    v1_ref, sa_ref, s_ref, rhs = rest
    m = own_ref.shape[0]
    half = v0_ref.shape[1] // 2
    far_rhs(rb_ref, rhs)

    zero = jnp.zeros((8, half), F32)
    acc = (zero,) * 3
    for i in range(m // step):
        rows = pl.ds(i * step, step)
        lhs = far_lhs(par_ref, l_ref, r_ref, rows)
        v1 = own_ref[rows, :] + jnp.dot(lhs, rhs[...], preferred_element_type=F32)
        v1_ref[rows, :] = v1
        ar, ai = v0_ref[rows, :half], v0_ref[rows, half:]
        br, bi = v1[:, :half], v1[:, half:]
        acc = (
            acc[0] + fold(br * ar + bi * ai),
            acc[1] + fold(br * ai - bi * ar),
            acc[2] + fold(br * br + bi * bi),
        )
    for k in range(3):
        s_ref[k : k + 1, :] = jnp.sum(acc[k], axis=0, keepdims=True)
    s_ref[3:, :] = jnp.zeros((5, half), F32)
    count = ida_ref.shape[0]
    bs = sa_ref.shape[0] // count
    for b in range(count):
        at = pl.ds(pl.multiple_of(ida_ref[b] * bs, bs), bs)
        sa_ref[b * bs : (b + 1) * bs] = v1_ref[at, :].astype(BF16)


def second_kernel(step, par_ref, own_ref, l_ref, r_ref, rb_ref, v0_ref, v1_ref, s1_ref, s_ref, rhs):
    m = own_ref.shape[0]
    half = v0_ref.shape[1] // 2
    far_rhs(rb_ref, rhs)

    zero = jnp.zeros((8, half), F32)
    acc = (zero,) * 5
    for i in range(m // step):
        rows = pl.ds(i * step, step)
        lhs = far_lhs(par_ref, l_ref, r_ref, rows)
        w = own_ref[rows, :] + jnp.dot(lhs, rhs[...], preferred_element_type=F32)
        ar, ai = v0_ref[rows, :half], v0_ref[rows, half:]
        br, bi = v1_ref[rows, :half], v1_ref[rows, half:]
        wr, wi = w[:, :half], w[:, half:]
        acc = (
            acc[0] + fold(wr * ar + wi * ai),
            acc[1] + fold(wr * ai - wi * ar),
            acc[2] + fold(wr * br + wi * bi),
            acc[3] + fold(wr * bi - wi * br),
            acc[4] + fold(wr * wr + wi * wi),
        )

    s_ref[...] = s1_ref[...]
    for k in range(5):
        s_ref[3 + k : 4 + k, :] = jnp.sum(acc[k], axis=0, keepdims=True)


def pick_kernel(dof_ref, v0_ref, v1_ref, out_ref, token_ref):
    token_ref[...] = jnp.zeros(token_ref.shape, F32)
    cols = v0_ref.shape[1]

    @pl.loop(0, out_ref.shape[0] // 8)
    def _(g):
        base = pl.multiple_of(g * 8, 8)
        at = [dof_ref[base + r] for r in range(8)]
        out_ref[pl.ds(base, 8), :cols] = jnp.concatenate(
            [v0_ref[pl.ds(a, 1), :] for a in at], axis=0
        )
        out_ref[pl.ds(base, 8), cols:] = jnp.concatenate(
            [v1_ref[pl.ds(a, 1), :] for a in at], axis=0
        )


def cmul(x, y):
    return x[0] * y[0] - x[1] * y[1], x[0] * y[1] + x[1] * y[0]


def resp_kernel(s_ref, motion_ref, pick_ref, r_ref, h_ref):
    half = s_ref.shape[1]
    row = lambda k: s_ref[k : k + 1, :]
    cross1, energy1 = (row(0), row(1)), row(2)
    a1 = tuple(c / (energy1 + EPSILON) for c in cross1)
    conj = (a1[0], -a1[1])
    wv0, wv1, ww = (row(3), row(4)), (row(5), row(6)), row(7)
    size = a1[0] * a1[0] + a1[1] * a1[1]
    p0, p1 = cmul(conj, wv0), cmul(conj, wv1)
    cross2 = tuple(a1[k] * EPSILON - p0[k] + size * wv1[k] for k in range(2))
    energy2 = jnp.maximum(energy1 - 2.0 * p1[0] + size * ww, 0.0)
    a2 = tuple(c / (energy2 + EPSILON) for c in cross2)
    both = cmul(a1, a2)
    h0 = (a1[0] + a2[0], a1[1] + a2[1])
    h1 = (-both[0], -both[1])
    h_ref[0:1], h_ref[1:2], h_ref[2:3], h_ref[3:4] = h0[0], h0[1], h1[0], h1[1]
    h_ref[4:] = jnp.zeros((4, half), F32)
    mo = (motion_ref[0:1, :half], motion_ref[0:1, half:])
    g0, g1 = cmul(h0, mo), cmul(h1, mo)
    chunk = 128
    for i in range(pick_ref.shape[0] // chunk):
        rows = slice(i * chunk, (i + 1) * chunk)
        re = im = None
        for t in range(half // 128):
            at = slice(t * 128, (t + 1) * 128)
            x = [pick_ref[rows, k * half + t * 128 : k * half + (t + 1) * 128] for k in range(4)]
            c = [g[:, at] for g in (*g0, *g1)]
            one = c[0] * x[0] - c[1] * x[1] + c[2] * x[2] - c[3] * x[3]
            two = c[0] * x[1] + c[1] * x[0] + c[2] * x[3] + c[3] * x[2]
            re = one if re is None else re + one
            im = two if im is None else im + two
        r_ref[0:1, rows] = jnp.sum(re.T, axis=0, keepdims=True)
        r_ref[1:2, rows] = jnp.sum(im.T, axis=0, keepdims=True)


def sol_kernel(h_ref, v0_ref, v1_ref, out_ref, buf, sems):
    chunks = sems.shape[0]
    half = h_ref.shape[1]
    rows = buf.shape[0] // chunks
    h = [h_ref[k : k + 1, :] for k in range(4)]
    for c in range(chunks):
        at = slice(c * rows, (c + 1) * rows)
        ar, ai = v0_ref[at, :half], v0_ref[at, half:]
        br, bi = v1_ref[at, :half], v1_ref[at, half:]
        buf[at, :half] = h[0] * ar - h[1] * ai + h[2] * br - h[3] * bi
        buf[at, half:] = h[0] * ai + h[1] * ar + h[2] * bi + h[3] * br
        pltpu.make_async_copy(
            buf.at[pl.ds(c * rows, rows)], out_ref.at[pl.ds(c * rows, rows)], sems.at[c]
        ).start()
    for c in range(chunks):
        pltpu.make_async_copy(
            buf.at[pl.ds(c * rows, rows)], out_ref.at[pl.ds(c * rows, rows)], sems.at[c]
        ).wait()


def table_kernel(fcount, f_ref, me_ref, load_ref, a_ref, _, out_ref, v0_ref, tile_ref, sems):
    chunks = sems.shape[0]
    copies = []
    for c in range(chunks):
        size = v0_ref.shape[0] // chunks
        rows = pl.ds(c * size, size)
        copies += [
            pltpu.make_async_copy(load_ref.at[rows], v0_ref.at[rows], sems.at[c, 0]),
            pltpu.make_async_copy(a_ref.at[0, rows], tile_ref.at[0, rows], sems.at[c, 1]),
            pltpu.make_async_copy(a_ref.at[1, rows], tile_ref.at[1, rows], sems.at[c, 2]),
        ]
    for copy in copies:
        copy.start()
    groups, nosc, lanes = out_ref.shape
    step = 128
    lane = lax.broadcasted_iota(jnp.int32, (groups, lanes), 1)
    of = (lane % (2 * fcount)) // 2
    wls = jnp.zeros((groups, lanes), F32)
    for p in range(fcount):
        wls = jnp.where(of == p, 2.0 * math.pi * f_ref[me_ref[0] ^ p], wls)
    number = lax.broadcasted_iota(jnp.int32, (groups, lanes), 0) * KGROUP + lane // (8 * fcount)
    phase = wls * (number.astype(F32) * TIME_STEP)
    cosine, sine = jnp.cos(phase), jnp.sin(phase)
    real = lane % 2 == 0
    xs, ys = jnp.where(real, cosine, -sine), jnp.where(real, -sine, -cosine)
    wl = wls[0:1]
    low = (lax.broadcasted_iota(jnp.int32, (step, lanes), 1) // (2 * fcount)) % 4 >= 2

    @pl.loop(0, nosc // step)
    def _(b):
        rows = pl.ds(pl.multiple_of(b * step, step), step)
        index = (lax.broadcasted_iota(jnp.int32, (step, lanes), 0) + b * step).astype(F32)
        osc = (2.0 * math.pi * 0.5) * jnp.exp(index * (math.log(100.0) / (nosc - 1)))
        stiffness = osc * osc
        damping = 2.0 * DAMPING * osc * wl
        detuning = stiffness - wl * wl
        scale = 1.0 / ((detuning * detuning + damping * damping) * fcount)
        gr = (stiffness * detuning + damping * damping) * scale
        gi = (damping * detuning - stiffness * damping) * scale
        for k in range(groups):
            value = xs[k : k + 1] * gr + ys[k : k + 1] * gi
            high = value.astype(BF16).astype(F32)
            out_ref[k, rows, :] = jnp.where(low, value - high, high).astype(BF16)

    for copy in copies:
        copy.wait()


def spec_kernel(step, me_ref, *rest):
    r_refs, (t_ref, out_ref, rhs) = rest[:-3], rest[-3:]
    groups, nosc, lanes = t_ref.shape
    nodes = out_ref.shape[0]
    per = lanes // KGROUP
    at = pl.ds(pl.multiple_of(me_ref[0] * nodes, nodes), nodes)
    r = jnp.concatenate([ref[:, at] for ref in r_refs], axis=0)
    high = r.astype(BF16).astype(F32)
    parts = jnp.concatenate([high, r - high, high, r - high], axis=0).astype(BF16)
    rhs[...] = jnp.zeros(rhs.shape, BF16)
    for k in range(KGROUP):
        rhs[k * per : (k + 1) * per, k * nodes : (k + 1) * nodes] = parts

    wide = 512
    for b in range(0, nosc, step):
        best = None
        for n in range(0, rhs.shape[1], wide):
            for g in range(groups):
                history = jnp.abs(
                    jnp.dot(
                        t_ref[g, b : b + step, :], rhs[:, n : n + wide], preferred_element_type=F32
                    )
                )
                for k in range(0, wide, nodes):
                    one = history[:, k : k + nodes]
                    best = one if best is None else jnp.maximum(best, one)
        out_ref[:, b : b + step] = best.T


def exchange(x, axis, count, bit):
    return lax.ppermute(x, axis, [(i, i ^ bit) for i in range(count)])


def total(x, axis):
    count = lax.axis_size(axis)
    if count & (count - 1):
        return lax.psum(x, axis)
    bit, radix = 1, 2
    while bit < count:
        radix = min(radix, count // bit)
        x = sum([exchange(x, axis, count, bit * k) for k in range(1, radix)], x)
        bit *= radix
        radix = 4
    return x


def everyone(x, axis):
    count = lax.axis_size(axis)
    return [x] + [exchange(x, axis, count, p) for p in range(1, count)]


def on_device(
    load,
    a_tile,
    left_tile,
    right_tile,
    block_mask,
    left_blocks,
    right_blocks,
    motion,
    freq_values,
    node_dof,
    node_owner,
):
    m, cols = load.shape[2:]
    half = cols // 2
    face = left_tile.shape[-1]
    bs = m // NB
    nsub, fcount = lax.axis_size("sub"), lax.axis_size("freq")
    sub, freq = lax.axis_index("sub"), lax.axis_index("freq")
    nodes_sub = node_dof.shape[1]
    nodes_own = nodes_sub // fcount
    parity = (sub % 2).astype(jnp.int32)
    even = parity == 0

    def swap_pairs(x, start):
        pairs = []
        for i in range(start, nsub - 1, 2):
            pairs += [(i, i + 1), (i + 1, i)]
        return lax.ppermute(x, "sub", pairs)

    near = functools.partial(swap_pairs, start=0)
    far = functools.partial(swap_pairs, start=1)

    left_ids, right_ids = left_blocks[0], right_blocks[0]
    send_b = far(jnp.where(even, left_ids, right_ids))
    send_a = near(jnp.where(even, right_ids, left_ids))

    load_h, tile_h, left_h, right_h = hbm(load[0, 0], a_tile[0, 0], left_tile[0, 0], right_tile[0, 0])

    packed = pltpu.VMEM((face, cols), BF16)
    token = jax.ShapeDtypeStruct((8, 128), F32)
    count = left_ids.shape[0]
    pack_a, pack_b = call(
        pack_kernel,
        (packed, packed),
        [SM, SM, HB],
        (VM, VM),
        [pltpu.VMEM((2, count, bs, cols), F32), pltpu.SemaphoreType.DMA((2, count))],
        limit=6,
    )(send_a, send_b, load_h)
    far1 = far(pack_b)
    near1 = near(pack_a)

    lanes = KGROUP * 8 * fcount
    me = freq.astype(jnp.int32).reshape(1)
    table, v0, tile = call(
        functools.partial(table_kernel, fcount),
        (
            pltpu.VMEM((NT // KGROUP, NOSC, lanes), BF16),
            pltpu.VMEM((m, cols), F32),
            pltpu.VMEM((2, m, m), BF16),
        ),
        [SM, SM, HB, HB, HB],
        (VM, VM, VM),
        [pltpu.SemaphoreType.DMA((3, 3))],
        limit=6,
    )(freq_values, me, load_h, tile_h, pack_b)
    v0, tile = vmem(v0, tile)

    mask = block_mask[0]
    parity1 = parity.reshape(1)

    def product(first, arrays, outs, sems):
        return call(
            functools.partial(own_kernel, first, 512),
            (pltpu.VMEM((m, cols), F32),) + outs,
            [SM, SM, VM] + ([HB] * 2 if first else [VM] * 2) + [VM, VM, HB],
            (VM,) * (1 + len(outs)),
            [pltpu.VMEM((2 * m + 2 * face, cols), BF16)] + sems,
            limit=14,
        )(mask, parity1, *arrays)

    side = pltpu.VMEM((2, m, face), BF16)
    own1, left, right = product(
        True,
        (tile, left_h, right_h, v0, *vmem(near1), pack_b),
        (side, side),
        [pltpu.SemaphoreType.DMA((m // 512, 2))],
    )
    left, right = vmem(left, right)

    rhs_scratch = pltpu.VMEM((2 * face, cols), BF16)
    pack_b2 = call(
        faces_kernel,
        packed,
        [SM, SM, VM, VM, VM, VM],
        VM,
        [rhs_scratch, pltpu.VMEM((face, 2 * face), BF16)],
        limit=6,
    )(send_b, parity1, *vmem(own1), left, right, *vmem(far1))
    far2 = far(pack_b2)

    v1, pack_a2, sums1 = call(
        functools.partial(image_kernel, 256),
        (pltpu.VMEM((m, cols), F32), packed, jax.ShapeDtypeStruct((8, half), F32)),
        [SM, SM, VM, VM, VM, VM, VM, HB],
        (VM, VM, VM),
        [rhs_scratch],
        limit=8,
    )(send_a, parity1, *vmem(own1), left, right, *vmem(far1), v0, pack_b2)
    near2 = near(pack_a2)

    owner, dof = node_owner[0], node_dof[0]
    number = jnp.arange(nodes_sub, dtype=jnp.int32)
    before = (owner[:, None] == owner[None, :]) & (number[None, :] < number[:, None])
    slot = owner * nodes_own + jnp.sum(before.astype(jnp.int32), axis=1)
    dof_of = jnp.sum(jnp.where(slot[None, :] == number[:, None], dof[None, :], 0), axis=1)
    picks, pick_token = call(
        pick_kernel,
        (pltpu.VMEM((nodes_sub, 2 * cols), F32), token),
        [SM, VM, VM],
        (VM, VM),
        limit=4,
    )(dof_of, v0, *vmem(v1))

    (own2,) = product(False, (tile, left, right, *vmem(v1, near2), pick_token), (), [])

    sums = call(
        functools.partial(second_kernel, 256),
        jax.ShapeDtypeStruct((8, half), F32),
        [SM] + [VM] * 7,
        VM,
        [rhs_scratch],
        limit=8,
    )(parity1, *vmem(own2), left, right, *vmem(far2), v0, *vmem(v1), sums1)
    sums = total(sums, "sub")

    resp, h = call(
        resp_kernel,
        (jax.ShapeDtypeStruct((2, nodes_sub), F32), jax.ShapeDtypeStruct((8, half), F32)),
        [VM, VM, VM],
        (VM, VM),
        limit=4,
    )(sums, motion, *vmem(picks))
    arrived = everyone(resp, "freq")
    solution = call(
        sol_kernel,
        jax.ShapeDtypeStruct((m, cols), F32),
        [VM, VM, VM],
        HB,
        [pltpu.VMEM((m, cols), F32), pltpu.SemaphoreType.DMA((6,))],
        limit=6,
    )(h, v0, *vmem(v1))

    spectra = call(
        functools.partial(spec_kernel, 256),
        jax.ShapeDtypeStruct((nodes_own, NOSC), F32),
        [SM] + [VM] * (fcount + 1),
        VM,
        [pltpu.VMEM((lanes, KGROUP * nodes_own), BF16)],
        limit=8,
    )(me, *arrived, *vmem(table))
    return solution[None, None], spectra[None]


def solution(mesh):
    placed = (
        P("sub", "freq", None, None),
        P("sub", "freq", None, None, None),
        P("sub", "freq", None, None, None),
        P("sub", "freq", None, None, None),
        P("sub", None, None),
        P("sub", None),
        P("sub", None),
        P("freq", None),
        P(),
        P("sub", None),
        P("sub", None),
    )
    return jax.shard_map(
        on_device,
        mesh=mesh,
        in_specs=placed,
        out_specs=(P("sub", "freq", None, None), P("sub", "freq", None)),
        check_vma=False,
    )
```

```python
import functools
import math

import jax
import jax.numpy as jnp
from jax import lax
from jax.experimental import pallas as pl
from jax.experimental.pallas import tpu as pltpu
from jax.sharding import PartitionSpec as P

NB = 12
NOSC = 1024
NT = 64
KGROUP = 8
EPSILON = 1e-06
DAMPING = 0.05
TIME_STEP = 0.01
MIB = 1024 * 1024

VM = pl.BlockSpec(memory_space=pltpu.VMEM)
SM = pl.BlockSpec(memory_space=pltpu.SMEM)
HB = pl.BlockSpec(memory_space=pl.ANY)
F32 = jnp.float32
BF16 = jnp.bfloat16


def hbm(*arrays):
    return [pltpu.with_memory_space_constraint(x, pltpu.HBM) for x in arrays]


def vmem(*arrays):
    return [pltpu.with_memory_space_constraint(x, pltpu.VMEM) for x in arrays]


def call(kernel, outs, in_specs, out_specs, scratch=(), limit=40, aliases=None):
    return pl.pallas_call(
        kernel,
        out_shape=outs,
        in_specs=in_specs,
        out_specs=out_specs,
        scratch_shapes=list(scratch),
        input_output_aliases=aliases or {},
        compiler_params=pltpu.CompilerParams(vmem_limit_bytes=limit * MIB),
    )


def turned(v):
    half = v.shape[-1] // 2
    return jnp.concatenate([-v[:, half:], v[:, :half]], axis=1)


def load_kernel(load_ref, v0_ref, sems):
    m = v0_ref.shape[0]
    chunks = sems.shape[0]
    size = m // chunks
    copies = []
    for c in range(chunks):
        rows = pl.ds(c * size, size)
        copies.append(pltpu.make_async_copy(load_ref.at[rows], v0_ref.at[rows], sems.at[c]))
    for copy in copies:
        copy.start()
    for copy in copies:
        copy.wait()


def pack_kernel(ida_ref, idb_ref, v0_ref, sa_ref, sb_ref):
    count = ida_ref.shape[0]
    rows = sa_ref.shape[0] // count
    for ids, out in ((idb_ref, sb_ref), (ida_ref, sa_ref)):
        for b in range(count):
            at = pl.ds(pl.multiple_of(ids[b] * rows, rows), rows)
            out[b * rows : (b + 1) * rows] = v0_ref[at].astype(BF16)


def own_kernel(first, step, mask_ref, par_ref, *rest):
    if first:
        sources, rest = rest[:3], rest[6:]
        v_ref, ra_ref, own_ref, a_ref, l_ref, r_ref, rhs, sems = rest
    else:
        a_ref, l_ref, r_ref, v_ref, ra_ref, own_ref, rhs = rest
    m, face = own_ref.shape[0], ra_ref.shape[0]
    bs = m // NB

    def fetch(i):
        rows = pl.ds(pl.multiple_of(i * step, step), step)
        return [
            pltpu.make_async_copy(source.at[c, rows], to.at[c, rows], sems.at[i - 1, k, c])
            for k, (source, to) in enumerate(zip(sources, (a_ref, l_ref, r_ref)))
            for c in range(2)
        ]

    if first:
        for i in range(1, m // step):
            for copy in fetch(i):
                copy.start()
    ra = ra_ref[...]
    rhs[0:face] = ra
    rhs[face:] = turned(ra)
    even = par_ref[0] == 0

    @pl.loop(0, m // step)
    def _(i):
        if first:

            @pl.when(i > 0)
            def _():
                for copy in fetch(i):
                    copy.wait()

        own, near = [], []
        for sub in range(step // bs):
            brow = i * (step // bs) + sub
            at = pl.ds(pl.multiple_of(i * step + sub * bs, bs), bs)
            keep = [(mask_ref[brow, j] != 0) | (brow == j) for j in range(NB)]
            pieces = []
            for c in range(2):
                for j in range(NB):
                    block = a_ref[c, at, j * bs : (j + 1) * bs]
                    pieces.append(lax.select(keep[j], block, jnp.zeros_like(block)))
            own.append(jnp.concatenate(pieces, axis=1))
            near.append(
                jnp.concatenate(
                    [lax.select(even, r_ref[c, at, :], l_ref[c, at, :]) for c in range(2)], axis=1
                )
            )
        rows = pl.ds(pl.multiple_of(i * step, step), step)
        out = jnp.dot(jnp.concatenate(own, axis=0), v_ref[...], preferred_element_type=F32)
        out += jnp.dot(jnp.concatenate(near, axis=0), rhs[...], preferred_element_type=F32)
        own_ref[rows, :] = out


def far_rhs(rb_ref, rhs):
    rb = rb_ref[...]
    face = rb.shape[0]
    rhs[0:face] = rb
    rhs[face:] = turned(rb)


def far_lhs(par_ref, l_ref, r_ref, rows):
    even = par_ref[0] == 0
    return jnp.concatenate(
        [lax.select(even, l_ref[c, rows, :], r_ref[c, rows, :]) for c in range(2)], axis=1
    )


def fold(x):
    return jnp.sum(x.reshape(x.shape[0] // 8, 8, x.shape[1]), axis=0)


def image_kernel(step, ida_ref, idb_ref, par_ref, own_ref, l_ref, r_ref, rb_ref, *rest):
    v1_ref, vb_ref, sa_ref, sb_ref, rhs = rest
    m = own_ref.shape[0]
    far_rhs(rb_ref, rhs)
    for i in range(m // step):
        rows = pl.ds(i * step, step)
        lhs = far_lhs(par_ref, l_ref, r_ref, rows)
        v1 = own_ref[rows, :] + jnp.dot(lhs, rhs[...], preferred_element_type=F32)
        v1_ref[rows, :] = v1
        vb = v1.astype(BF16)
        vb_ref[rows, :] = vb
        vb_ref[pl.ds(m + i * step, step), :] = turned(vb)
    count = ida_ref.shape[0]
    bs = sa_ref.shape[0] // count
    for ids, out in ((idb_ref, sb_ref), (ida_ref, sa_ref)):
        for b in range(count):
            at = pl.ds(pl.multiple_of(ids[b] * bs, bs), bs)
            out[b * bs : (b + 1) * bs] = vb_ref[at, :]


def sums_kernel(step, v0_ref, v1_ref, s_ref):
    m = v0_ref.shape[0]
    half = v0_ref.shape[1] // 2
    zero = jnp.zeros((8, half), F32)
    acc = (zero,) * 3
    for i in range(m // step):
        rows = pl.ds(i * step, step)
        ar, ai = v0_ref[rows, :half], v0_ref[rows, half:]
        br, bi = v1_ref[rows, :half], v1_ref[rows, half:]
        acc = (
            acc[0] + fold(br * ar + bi * ai),
            acc[1] + fold(br * ai - bi * ar),
            acc[2] + fold(br * br + bi * bi),
        )
    for k in range(3):
        s_ref[k : k + 1, :] = jnp.sum(acc[k], axis=0, keepdims=True)
    s_ref[3:, :] = jnp.zeros((5, half), F32)


def second_kernel(step, par_ref, own_ref, l_ref, r_ref, rb_ref, v0_ref, v1_ref, s1_ref, _, s_ref, rhs):
    m = own_ref.shape[0]
    half = v0_ref.shape[1] // 2
    far_rhs(rb_ref, rhs)

    zero = jnp.zeros((8, half), F32)
    acc = (zero,) * 5
    for i in range(m // step):
        rows = pl.ds(i * step, step)
        lhs = far_lhs(par_ref, l_ref, r_ref, rows)
        w = own_ref[rows, :] + jnp.dot(lhs, rhs[...], preferred_element_type=F32)
        ar, ai = v0_ref[rows, :half], v0_ref[rows, half:]
        br, bi = v1_ref[rows, :half], v1_ref[rows, half:]
        wr, wi = w[:, :half], w[:, half:]
        acc = (
            acc[0] + fold(wr * ar + wi * ai),
            acc[1] + fold(wr * ai - wi * ar),
            acc[2] + fold(wr * br + wi * bi),
            acc[3] + fold(wr * bi - wi * br),
            acc[4] + fold(wr * wr + wi * wi),
        )

    s_ref[...] = s1_ref[...]
    for k in range(5):
        s_ref[3 + k : 4 + k, :] = jnp.sum(acc[k], axis=0, keepdims=True)


def pick_kernel(dof_ref, v0_ref, v1_ref, out_ref):
    cols = v0_ref.shape[1]

    @pl.loop(0, out_ref.shape[0] // 8)
    def _(g):
        base = pl.multiple_of(g * 8, 8)
        at = [dof_ref[base + r] for r in range(8)]
        for k, v_ref in enumerate((v0_ref, v1_ref)):
            out_ref[pl.ds(base, 8), k * cols : (k + 1) * cols] = jnp.concatenate(
                [v_ref[pl.ds(a, 1), :] for a in at], axis=0
            )


def cmul(x, y):
    return x[0] * y[0] - x[1] * y[1], x[0] * y[1] + x[1] * y[0]


def resp_kernel(s_ref, motion_ref, pick_ref, r_ref, h_ref):
    half = s_ref.shape[1]
    row = lambda k: s_ref[k : k + 1, :]
    cross1, energy1 = (row(0), row(1)), row(2)
    a1 = tuple(c / (energy1 + EPSILON) for c in cross1)
    conj = (a1[0], -a1[1])
    wv0, wv1, ww = (row(3), row(4)), (row(5), row(6)), row(7)
    size = a1[0] * a1[0] + a1[1] * a1[1]
    p0, p1 = cmul(conj, wv0), cmul(conj, wv1)
    cross2 = tuple(a1[k] * EPSILON - p0[k] + size * wv1[k] for k in range(2))
    energy2 = jnp.maximum(energy1 - 2.0 * p1[0] + size * ww, 0.0)
    a2 = tuple(c / (energy2 + EPSILON) for c in cross2)
    both = cmul(a1, a2)
    h0 = (a1[0] + a2[0], a1[1] + a2[1])
    h1 = (-both[0], -both[1])
    h_ref[0:1], h_ref[1:2], h_ref[2:3], h_ref[3:4] = h0[0], h0[1], h1[0], h1[1]
    h_ref[4:] = jnp.zeros((4, half), F32)
    mo = (motion_ref[0:1, :half], motion_ref[0:1, half:])
    g0, g1 = cmul(h0, mo), cmul(h1, mo)
    chunk = 128
    for i in range(pick_ref.shape[0] // chunk):
        rows = slice(i * chunk, (i + 1) * chunk)
        re = im = None
        for t in range(half // 128):
            at = slice(t * 128, (t + 1) * 128)
            x = [pick_ref[rows, k * half + t * 128 : k * half + (t + 1) * 128] for k in range(4)]
            c = [g[:, at] for g in (*g0, *g1)]
            one = c[0] * x[0] - c[1] * x[1] + c[2] * x[2] - c[3] * x[3]
            two = c[0] * x[1] + c[1] * x[0] + c[2] * x[3] + c[3] * x[2]
            re = one if re is None else re + one
            im = two if im is None else im + two
        r_ref[0:1, rows] = jnp.sum(re.T, axis=0, keepdims=True)
        r_ref[1:2, rows] = jnp.sum(im.T, axis=0, keepdims=True)


def sol_kernel(h_ref, v0_ref, v1_ref, out_ref, buf, sems):
    chunks = sems.shape[0]
    half = h_ref.shape[1]
    rows = buf.shape[0] // chunks
    h = [h_ref[k : k + 1, :] for k in range(4)]
    for c in range(chunks):
        at = slice(c * rows, (c + 1) * rows)
        ar, ai = v0_ref[at, :half], v0_ref[at, half:]
        br, bi = v1_ref[at, :half], v1_ref[at, half:]
        buf[at, :half] = h[0] * ar - h[1] * ai + h[2] * br - h[3] * bi
        buf[at, half:] = h[0] * ai + h[1] * ar + h[2] * bi + h[3] * br
        pltpu.make_async_copy(
            buf.at[pl.ds(c * rows, rows)], out_ref.at[pl.ds(c * rows, rows)], sems.at[c]
        ).start()
    for c in range(chunks):
        pltpu.make_async_copy(
            buf.at[pl.ds(c * rows, rows)], out_ref.at[pl.ds(c * rows, rows)], sems.at[c]
        ).wait()


def table_kernel(fcount, first, f_ref, me_ref, *rest):
    sources, v0_ref, out_ref, vb_ref, tiles, sems = rest[:3], rest[4], *rest[5:7], rest[7:10], rest[10]
    copies = []
    for k in range(3):
        for c in range(2):
            rows = pl.ds(0, first)
            copies.append(
                pltpu.make_async_copy(
                    sources[k].at[c, rows], tiles[k].at[c, rows], sems.at[k, c]
                )
            )
    for copy in copies:
        copy.start()
    groups, nosc, lanes = out_ref.shape
    step = 128
    lane = lax.broadcasted_iota(jnp.int32, (groups, lanes), 1)
    of = (lane % (2 * fcount)) // 2
    wls = jnp.zeros((groups, lanes), F32)
    for p in range(fcount):
        wls = jnp.where(of == p, 2.0 * math.pi * f_ref[me_ref[0] ^ p], wls)
    number = lax.broadcasted_iota(jnp.int32, (groups, lanes), 0) * KGROUP + lane // (8 * fcount)
    phase = wls * (number.astype(F32) * TIME_STEP)
    cosine, sine = jnp.cos(phase), jnp.sin(phase)
    real = lane % 2 == 0
    xs, ys = jnp.where(real, cosine, -sine), jnp.where(real, -sine, -cosine)
    wl = wls[0:1]
    low = (lax.broadcasted_iota(jnp.int32, (step, lanes), 1) // (2 * fcount)) % 4 >= 2

    @pl.loop(0, nosc // step)
    def _(b):
        rows = pl.ds(pl.multiple_of(b * step, step), step)
        index = (lax.broadcasted_iota(jnp.int32, (step, lanes), 0) + b * step).astype(F32)
        osc = (2.0 * math.pi * 0.5) * jnp.exp(index * (math.log(100.0) / (nosc - 1)))
        stiffness = osc * osc
        damping = 2.0 * DAMPING * osc * wl
        detuning = stiffness - wl * wl
        scale = 1.0 / ((detuning * detuning + damping * damping) * fcount)
        gr = (stiffness * detuning + damping * damping) * scale
        gi = (damping * detuning - stiffness * damping) * scale
        for k in range(groups):
            value = xs[k : k + 1] * gr + ys[k : k + 1] * gi
            high = value.astype(BF16).astype(F32)
            out_ref[k, rows, :] = jnp.where(low, value - high, high).astype(BF16)

    m = v0_ref.shape[0]
    vb = v0_ref[...].astype(BF16)
    vb_ref[0:m] = vb
    vb_ref[m:] = turned(vb)
    for copy in copies:
        copy.wait()


def spec_kernel(step, me_ref, *rest):
    r_refs, (t_ref, out_ref, rhs) = rest[:-3], rest[-3:]
    groups, nosc, lanes = t_ref.shape
    nodes = out_ref.shape[0]
    per = lanes // KGROUP
    at = pl.ds(pl.multiple_of(me_ref[0] * nodes, nodes), nodes)
    r = jnp.concatenate([ref[:, at] for ref in r_refs], axis=0)
    high = r.astype(BF16).astype(F32)
    parts = jnp.concatenate([high, r - high, high, r - high], axis=0).astype(BF16)
    rhs[...] = jnp.zeros(rhs.shape, BF16)
    for k in range(KGROUP):
        rhs[k * per : (k + 1) * per, k * nodes : (k + 1) * nodes] = parts

    wide = 512
    for b in range(0, nosc, step):
        best = None
        for n in range(0, rhs.shape[1], wide):
            for g in range(groups):
                history = jnp.abs(
                    jnp.dot(
                        t_ref[g, b : b + step, :], rhs[:, n : n + wide], preferred_element_type=F32
                    )
                )
                for k in range(0, wide, nodes):
                    one = history[:, k : k + nodes]
                    best = one if best is None else jnp.maximum(best, one)
        out_ref[:, b : b + step] = best.T


def exchange(x, axis, count, bit):
    return lax.ppermute(x, axis, [(i, i ^ bit) for i in range(count)])


def total(x, axis):
    count = lax.axis_size(axis)
    if count & (count - 1):
        return lax.psum(x, axis)
    bit = 1
    while bit < count:
        x = x + exchange(x, axis, count, bit)
        bit *= 2
    return x


def everyone(x, axis):
    count = lax.axis_size(axis)
    if count & (count - 1):
        return jnp.concatenate([x] + [exchange(x, axis, count, p) for p in range(1, count)], axis=0)
    bit = 1
    while bit < count:
        x = jnp.concatenate([x, exchange(x, axis, count, bit)], axis=0)
        bit *= 2
    return x


def on_device(
    load,
    a_tile,
    left_tile,
    right_tile,
    block_mask,
    left_blocks,
    right_blocks,
    motion,
    freq_values,
    node_dof,
    node_owner,
):
    m, cols = load.shape[2:]
    half = cols // 2
    face = left_tile.shape[-1]
    bs = m // NB
    nsub, fcount = lax.axis_size("sub"), lax.axis_size("freq")
    sub, freq = lax.axis_index("sub"), lax.axis_index("freq")
    nodes_sub = node_dof.shape[1]
    nodes_own = nodes_sub // fcount
    parity = (sub % 2).astype(jnp.int32)
    even = parity == 0

    def swap_pairs(x, start):
        pairs = []
        for i in range(start, nsub - 1, 2):
            pairs += [(i, i + 1), (i + 1, i)]
        return lax.ppermute(x, "sub", pairs)

    near = functools.partial(swap_pairs, start=0)
    far = functools.partial(swap_pairs, start=1)

    left_ids, right_ids = left_blocks[0], right_blocks[0]
    send_b = far(jnp.where(even, left_ids, right_ids))
    send_a = near(jnp.where(even, right_ids, left_ids))

    load_h, tile_h, left_h, right_h = hbm(load[0, 0], a_tile[0, 0], left_tile[0, 0], right_tile[0, 0])

    packed = pltpu.VMEM((face, cols), BF16)
    doubled = pltpu.VMEM((2 * m, cols), BF16)
    (v0,) = vmem(
        call(
            load_kernel,
            pltpu.VMEM((m, cols), F32),
            [HB],
            VM,
            [pltpu.SemaphoreType.DMA((6,))],
            limit=4,
        )(load_h)
    )
    pack_a, pack_b = call(pack_kernel, (packed, packed), [SM, SM, VM], (VM, VM), limit=4)(
        send_a, send_b, v0
    )
    far1 = far(pack_b)
    near1 = near(pack_a)

    lanes = KGROUP * 8 * fcount
    me = freq.astype(jnp.int32).reshape(1)
    step = m // 3
    tile_shape, side = pltpu.VMEM((2, m, m), BF16), pltpu.VMEM((2, m, face), BF16)
    table, v0b, *tiles = call(
        functools.partial(table_kernel, fcount, step),
        (
            pltpu.VMEM((NT // KGROUP, NOSC, lanes), BF16),
            doubled,
            tile_shape,
            side,
            side,
        ),
        [SM, SM] + [HB] * 4 + [VM],
        (VM,) * 5,
        [pltpu.SemaphoreType.DMA((3, 2))],
        limit=6,
    )(freq_values, me, tile_h, left_h, right_h, pack_b, v0)

    mask = block_mask[0]
    parity1 = parity.reshape(1)
    image_shape = pltpu.VMEM((m, cols), F32)
    near_rhs = pltpu.VMEM((2 * face, cols), BF16)
    own1, tile, left, right = call(
        functools.partial(own_kernel, True, step),
        (image_shape, tile_shape, side, side),
        [SM, SM] + [HB] * 3 + [VM] * 5,
        (VM,) * 4,
        [near_rhs, pltpu.SemaphoreType.DMA((m // step - 1, 3, 2))],
        limit=10,
        aliases={5: 1, 6: 2, 7: 3},
    )(mask, parity1, tile_h, left_h, right_h, *vmem(*tiles, v0b, near1))
    tile, left, right = vmem(tile, left, right)

    rhs_scratch = pltpu.VMEM((2 * face, cols), BF16)
    v1, v1b, pack_a2, pack_b2 = call(
        functools.partial(image_kernel, 512),
        (image_shape, doubled, packed, packed),
        [SM, SM, SM, VM, VM, VM, VM],
        (VM, VM, VM, VM),
        [rhs_scratch],
        limit=8,
    )(send_a, send_b, parity1, *vmem(own1), left, right, *vmem(far1))
    far2 = far(pack_b2)
    near2 = near(pack_a2)
    (v1,) = vmem(v1)
    sums1 = call(
        functools.partial(sums_kernel, 128),
        jax.ShapeDtypeStruct((8, half), F32),
        [VM, VM],
        VM,
        limit=4,
    )(v0, v1)

    own2 = call(
        functools.partial(own_kernel, False, step),
        image_shape,
        [SM, SM] + [VM] * 5,
        VM,
        [near_rhs],
        limit=10,
    )(mask, parity1, tile, left, right, *vmem(v1b, near2))

    owner, dof = node_owner[0], node_dof[0]
    number = jnp.arange(nodes_sub, dtype=jnp.int32)
    before = (owner[:, None] == owner[None, :]) & (number[None, :] < number[:, None])
    slot = owner * nodes_own + jnp.sum(before.astype(jnp.int32), axis=1)
    dof_of = jnp.sum(jnp.where(slot[None, :] == number[:, None], dof[None, :], 0), axis=1)
    picks = call(
        pick_kernel,
        pltpu.VMEM((nodes_sub, 2 * cols), F32),
        [SM, VM, VM],
        VM,
        limit=4,
    )(dof_of, v0, v1)

    sums = call(
        functools.partial(second_kernel, 256),
        jax.ShapeDtypeStruct((8, half), F32),
        [SM] + [VM] * 7 + [HB],
        VM,
        [rhs_scratch],
        limit=8,
    )(parity1, *vmem(own2), left, right, *vmem(far2), v0, v1, sums1, picks)

    sums = total(sums, "sub")

    resp, h = call(
        resp_kernel,
        (jax.ShapeDtypeStruct((2, nodes_sub), F32), jax.ShapeDtypeStruct((8, half), F32)),
        [VM, VM, VM],
        (VM, VM),
        limit=4,
    )(sums, motion, *vmem(picks))
    arrived = everyone(resp, "freq")
    solution = call(
        sol_kernel,
        jax.ShapeDtypeStruct((m, cols), F32),
        [VM, VM, VM],
        HB,
        [pltpu.VMEM((m, cols), F32), pltpu.SemaphoreType.DMA((6,))],
        limit=6,
    )(h, v0, *vmem(v1))

    spectra = call(
        functools.partial(spec_kernel, 256),
        jax.ShapeDtypeStruct((nodes_own, NOSC), F32),
        [SM, VM, VM],
        VM,
        [pltpu.VMEM((lanes, KGROUP * nodes_own), BF16)],
        limit=8,
    )(me, arrived, *vmem(table))
    return solution[None, None], spectra[None]


def solution(mesh):
    placed = (
        P("sub", "freq", None, None),
        P("sub", "freq", None, None, None),
        P("sub", "freq", None, None, None),
        P("sub", "freq", None, None, None),
        P("sub", None, None),
        P("sub", None),
        P("sub", None),
        P("freq", None),
        P(),
        P("sub", None),
        P("sub", None),
    )
    return jax.shard_map(
        on_device,
        mesh=mesh,
        in_specs=placed,
        out_specs=(P("sub", "freq", None, None), P("sub", "freq", None)),
        check_vma=False,
    )
```

```python
import functools
import math

import jax
import jax.numpy as jnp
from jax import lax
from jax.experimental import pallas as pl
from jax.experimental.pallas import tpu as pltpu
from jax.sharding import PartitionSpec as P

NB = 12
NOSC = 1024
NT = 64
KGROUP = 8
EPSILON = 1e-06
DAMPING = 0.05
TIME_STEP = 0.01
MIB = 1024 * 1024

VM = pl.BlockSpec(memory_space=pltpu.VMEM)
SM = pl.BlockSpec(memory_space=pltpu.SMEM)
HB = pl.BlockSpec(memory_space=pl.ANY)
F32 = jnp.float32
BF16 = jnp.bfloat16


def hbm(*arrays):
    return [pltpu.with_memory_space_constraint(x, pltpu.HBM) for x in arrays]


def vmem(*arrays):
    return [pltpu.with_memory_space_constraint(x, pltpu.VMEM) for x in arrays]


def call(kernel, outs, in_specs, out_specs, scratch=(), limit=40, aliases=None):
    return pl.pallas_call(
        kernel,
        out_shape=outs,
        in_specs=in_specs,
        out_specs=out_specs,
        scratch_shapes=list(scratch),
        input_output_aliases=aliases or {},
        compiler_params=pltpu.CompilerParams(vmem_limit_bytes=limit * MIB),
    )


def turned(v):
    half = v.shape[-1] // 2
    return jnp.concatenate([-v[:, half:], v[:, :half]], axis=1)


def load_kernel(load_ref, v0_ref, sems):
    m = v0_ref.shape[0]
    chunks = sems.shape[0]
    size = m // chunks
    copies = []
    for c in range(chunks):
        rows = pl.ds(c * size, size)
        copies.append(pltpu.make_async_copy(load_ref.at[rows], v0_ref.at[rows], sems.at[c]))
    for copy in copies:
        copy.start()
    for copy in copies:
        copy.wait()


def pack_kernel(ida_ref, idb_ref, v0_ref, sa_ref, sb_ref, buf, sems):
    count = ida_ref.shape[0]
    rows = sa_ref.shape[0] // count
    copies = []
    for k, (ids, out) in enumerate(((idb_ref, sb_ref), (ida_ref, sa_ref))):
        for b in range(count):
            at = pl.ds(pl.multiple_of(ids[b] * rows, rows), rows)
            buf[k, b] = v0_ref[at].astype(BF16)
            copies.append(
                pltpu.make_async_copy(buf.at[k, b], out.at[pl.ds(b * rows, rows)], sems.at[k, b])
            )
            copies[-1].start()
    for copy in copies:
        copy.wait()


def own_kernel(first, step, mask_ref, par_ref, *rest):
    if first:
        sources, rest = rest[:3], rest[6:]
        v_ref, ra_ref, own_ref, a_ref, l_ref, r_ref, rhs, sems = rest
    else:
        a_ref, l_ref, r_ref, v_ref, ra_ref, own_ref, rhs = rest
    m, face = own_ref.shape[0], ra_ref.shape[0]
    bs = m // NB

    def fetch(i):
        rows = pl.ds(pl.multiple_of(i * step, step), step)
        return [
            pltpu.make_async_copy(source.at[c, rows], to.at[c, rows], sems.at[i - 1, k, c])
            for k, (source, to) in enumerate(zip(sources, (a_ref, l_ref, r_ref)))
            for c in range(2)
        ]

    if first:
        for i in range(1, m // step):
            for copy in fetch(i):
                copy.start()
    ra = ra_ref[...]
    rhs[0:face] = ra
    rhs[face:] = turned(ra)
    even = par_ref[0] == 0

    @pl.loop(0, m // step)
    def _(i):
        if first:

            @pl.when(i > 0)
            def _():
                for copy in fetch(i):
                    copy.wait()

        own, near = [], []
        for sub in range(step // bs):
            brow = i * (step // bs) + sub
            at = pl.ds(pl.multiple_of(i * step + sub * bs, bs), bs)
            keep = [(mask_ref[brow, j] != 0) | (brow == j) for j in range(NB)]
            pieces = []
            for c in range(2):
                for j in range(NB):
                    block = a_ref[c, at, j * bs : (j + 1) * bs]
                    pieces.append(lax.select(keep[j], block, jnp.zeros_like(block)))
            own.append(jnp.concatenate(pieces, axis=1))
            near.append(
                jnp.concatenate(
                    [lax.select(even, r_ref[c, at, :], l_ref[c, at, :]) for c in range(2)], axis=1
                )
            )
        rows = pl.ds(pl.multiple_of(i * step, step), step)
        out = jnp.dot(jnp.concatenate(own, axis=0), v_ref[...], preferred_element_type=F32)
        out += jnp.dot(jnp.concatenate(near, axis=0), rhs[...], preferred_element_type=F32)
        own_ref[rows, :] = out


def far_rhs(rb_ref, rhs):
    rb = rb_ref[...]
    face = rb.shape[0]
    rhs[0:face] = rb
    rhs[face:] = turned(rb)


def far_lhs(par_ref, l_ref, r_ref, rows):
    even = par_ref[0] == 0
    return jnp.concatenate(
        [lax.select(even, l_ref[c, rows, :], r_ref[c, rows, :]) for c in range(2)], axis=1
    )


def fold(x):
    return jnp.sum(x.reshape(x.shape[0] // 8, 8, x.shape[1]), axis=0)


def faces_kernel(ida_ref, idb_ref, par_ref, own_ref, l_ref, r_ref, rb_ref, *rest):
    sa_ref, sb_ref, token_ref, rhs, lhs = rest
    token_ref[...] = jnp.zeros(token_ref.shape, F32)
    count = ida_ref.shape[0]
    rows = sa_ref.shape[0] // count
    far_rhs(rb_ref, rhs)
    ats = [
        pl.ds(pl.multiple_of(ids[b] * rows, rows), rows)
        for ids in (idb_ref, ida_ref)
        for b in range(count)
    ]
    for k, at in enumerate(ats):
        lhs[k * rows : (k + 1) * rows] = far_lhs(par_ref, l_ref, r_ref, at)
    part = jnp.dot(lhs[...], rhs[...], preferred_element_type=F32)
    for k, at in enumerate(ats):
        out = (own_ref[at, :] + part[k * rows : (k + 1) * rows]).astype(BF16)
        to = (k % count) * rows
        (sb_ref if k < count else sa_ref)[to : to + rows] = out


def image_kernel(step, par_ref, own_ref, l_ref, r_ref, rb_ref, _, v1_ref, vb_ref, rhs):
    m = own_ref.shape[0]
    far_rhs(rb_ref, rhs)
    for i in range(m // step):
        rows = pl.ds(i * step, step)
        lhs = far_lhs(par_ref, l_ref, r_ref, rows)
        v1 = own_ref[rows, :] + jnp.dot(lhs, rhs[...], preferred_element_type=F32)
        v1_ref[rows, :] = v1
        vb = v1.astype(BF16)
        vb_ref[rows, :] = vb
        vb_ref[pl.ds(m + i * step, step), :] = turned(vb)


def sums_kernel(step, v0_ref, v1_ref, s_ref):
    m = v0_ref.shape[0]
    half = v0_ref.shape[1] // 2
    zero = jnp.zeros((8, half), F32)
    acc = (zero,) * 3
    for i in range(m // step):
        rows = pl.ds(i * step, step)
        ar, ai = v0_ref[rows, :half], v0_ref[rows, half:]
        br, bi = v1_ref[rows, :half], v1_ref[rows, half:]
        acc = (
            acc[0] + fold(br * ar + bi * ai),
            acc[1] + fold(br * ai - bi * ar),
            acc[2] + fold(br * br + bi * bi),
        )
    for k in range(3):
        s_ref[k : k + 1, :] = jnp.sum(acc[k], axis=0, keepdims=True)
    s_ref[3:, :] = jnp.zeros((5, half), F32)


def second_kernel(step, par_ref, own_ref, l_ref, r_ref, rb_ref, v0_ref, v1_ref, s1_ref, s_ref, rhs):
    m = own_ref.shape[0]
    half = v0_ref.shape[1] // 2
    far_rhs(rb_ref, rhs)

    zero = jnp.zeros((8, half), F32)
    acc = (zero,) * 5
    for i in range(m // step):
        rows = pl.ds(i * step, step)
        lhs = far_lhs(par_ref, l_ref, r_ref, rows)
        w = own_ref[rows, :] + jnp.dot(lhs, rhs[...], preferred_element_type=F32)
        ar, ai = v0_ref[rows, :half], v0_ref[rows, half:]
        br, bi = v1_ref[rows, :half], v1_ref[rows, half:]
        wr, wi = w[:, :half], w[:, half:]
        acc = (
            acc[0] + fold(wr * ar + wi * ai),
            acc[1] + fold(wr * ai - wi * ar),
            acc[2] + fold(wr * br + wi * bi),
            acc[3] + fold(wr * bi - wi * br),
            acc[4] + fold(wr * wr + wi * wi),
        )

    s_ref[...] = s1_ref[...]
    for k in range(5):
        s_ref[3 + k : 4 + k, :] = jnp.sum(acc[k], axis=0, keepdims=True)


def pick_kernel(first, dof_ref, v0_ref, v1_ref, s_ref, out_ref, again_ref):
    again_ref[...] = s_ref[...]
    cols = v0_ref.shape[1]

    @pl.loop(0, out_ref.shape[0] // 8)
    def _(g):
        base = pl.multiple_of(g * 8, 8)
        at = [dof_ref[first + base + r] for r in range(8)]
        for k, v_ref in enumerate((v0_ref, v1_ref)):
            out_ref[pl.ds(base, 8), k * cols : (k + 1) * cols] = jnp.concatenate(
                [v_ref[pl.ds(a, 1), :] for a in at], axis=0
            )


def cmul(x, y):
    return x[0] * y[0] - x[1] * y[1], x[0] * y[1] + x[1] * y[0]


def resp_kernel(s_ref, motion_ref, p0_ref, p1_ref, r_ref, h_ref):
    half = s_ref.shape[1]
    row = lambda k: s_ref[k : k + 1, :]
    cross1, energy1 = (row(0), row(1)), row(2)
    a1 = tuple(c / (energy1 + EPSILON) for c in cross1)
    conj = (a1[0], -a1[1])
    wv0, wv1, ww = (row(3), row(4)), (row(5), row(6)), row(7)
    size = a1[0] * a1[0] + a1[1] * a1[1]
    p0, p1 = cmul(conj, wv0), cmul(conj, wv1)
    cross2 = tuple(a1[k] * EPSILON - p0[k] + size * wv1[k] for k in range(2))
    energy2 = jnp.maximum(energy1 - 2.0 * p1[0] + size * ww, 0.0)
    a2 = tuple(c / (energy2 + EPSILON) for c in cross2)
    both = cmul(a1, a2)
    h0 = (a1[0] + a2[0], a1[1] + a2[1])
    h1 = (-both[0], -both[1])
    h_ref[0:1], h_ref[1:2], h_ref[2:3], h_ref[3:4] = h0[0], h0[1], h1[0], h1[1]
    h_ref[4:] = jnp.zeros((4, half), F32)
    mo = (motion_ref[0:1, :half], motion_ref[0:1, half:])
    g0, g1 = cmul(h0, mo), cmul(h1, mo)
    chunk = 128
    part = p0_ref.shape[0] // chunk
    for i in range(2 * part):
        pick_ref = p0_ref if i < part else p1_ref
        rows = slice(i % part * chunk, (i % part + 1) * chunk)
        to = slice(i * chunk, (i + 1) * chunk)
        re = im = None
        for t in range(half // 128):
            at = slice(t * 128, (t + 1) * 128)
            x = [pick_ref[rows, k * half + t * 128 : k * half + (t + 1) * 128] for k in range(4)]
            c = [g[:, at] for g in (*g0, *g1)]
            one = c[0] * x[0] - c[1] * x[1] + c[2] * x[2] - c[3] * x[3]
            two = c[0] * x[1] + c[1] * x[0] + c[2] * x[3] + c[3] * x[2]
            re = one if re is None else re + one
            im = two if im is None else im + two
        r_ref[0:1, to] = jnp.sum(re.T, axis=0, keepdims=True)
        r_ref[1:2, to] = jnp.sum(im.T, axis=0, keepdims=True)


def sol_kernel(h_ref, v0_ref, v1_ref, out_ref, buf, sems):
    chunks = sems.shape[0]
    half = h_ref.shape[1]
    rows = buf.shape[0] // chunks
    h = [h_ref[k : k + 1, :] for k in range(4)]
    for c in range(chunks):
        at = slice(c * rows, (c + 1) * rows)
        ar, ai = v0_ref[at, :half], v0_ref[at, half:]
        br, bi = v1_ref[at, :half], v1_ref[at, half:]
        buf[at, :half] = h[0] * ar - h[1] * ai + h[2] * br - h[3] * bi
        buf[at, half:] = h[0] * ai + h[1] * ar + h[2] * bi + h[3] * br
        pltpu.make_async_copy(
            buf.at[pl.ds(c * rows, rows)], out_ref.at[pl.ds(c * rows, rows)], sems.at[c]
        ).start()
    for c in range(chunks):
        pltpu.make_async_copy(
            buf.at[pl.ds(c * rows, rows)], out_ref.at[pl.ds(c * rows, rows)], sems.at[c]
        ).wait()


def table_kernel(fcount, first, f_ref, me_ref, *rest):
    sources, v0_ref, out_ref, vb_ref, tiles, sems = rest[:3], rest[4], *rest[5:7], rest[7:10], rest[10]
    copies = []
    for k in range(3):
        for c in range(2):
            rows = pl.ds(0, first)
            copies.append(
                pltpu.make_async_copy(
                    sources[k].at[c, rows], tiles[k].at[c, rows], sems.at[k, c]
                )
            )
    for copy in copies:
        copy.start()
    groups, nosc, lanes = out_ref.shape
    step = 128
    lane = lax.broadcasted_iota(jnp.int32, (groups, lanes), 1)
    of = (lane % (2 * fcount)) // 2
    wls = jnp.zeros((groups, lanes), F32)
    for p in range(fcount):
        wls = jnp.where(of == p, 2.0 * math.pi * f_ref[me_ref[0] ^ p], wls)
    number = lax.broadcasted_iota(jnp.int32, (groups, lanes), 0) * KGROUP + lane // (8 * fcount)
    phase = wls * (number.astype(F32) * TIME_STEP)
    cosine, sine = jnp.cos(phase), jnp.sin(phase)
    real = lane % 2 == 0
    xs, ys = jnp.where(real, cosine, -sine), jnp.where(real, -sine, -cosine)
    wl = wls[0:1]
    low = (lax.broadcasted_iota(jnp.int32, (step, lanes), 1) // (2 * fcount)) % 4 >= 2

    @pl.loop(0, nosc // step)
    def _(b):
        rows = pl.ds(pl.multiple_of(b * step, step), step)
        index = (lax.broadcasted_iota(jnp.int32, (step, lanes), 0) + b * step).astype(F32)
        osc = (2.0 * math.pi * 0.5) * jnp.exp(index * (math.log(100.0) / (nosc - 1)))
        stiffness = osc * osc
        damping = 2.0 * DAMPING * osc * wl
        detuning = stiffness - wl * wl
        scale = 1.0 / ((detuning * detuning + damping * damping) * fcount)
        gr = (stiffness * detuning + damping * damping) * scale
        gi = (damping * detuning - stiffness * damping) * scale
        for k in range(groups):
            value = xs[k : k + 1] * gr + ys[k : k + 1] * gi
            high = value.astype(BF16).astype(F32)
            out_ref[k, rows, :] = jnp.where(low, value - high, high).astype(BF16)

    m = v0_ref.shape[0]
    vb = v0_ref[...].astype(BF16)
    vb_ref[0:m] = vb
    vb_ref[m:] = turned(vb)
    for copy in copies:
        copy.wait()


def spec_kernel(step, me_ref, *rest):
    r_refs, (t_ref, out_ref, rhs) = rest[:-3], rest[-3:]
    groups, nosc, lanes = t_ref.shape
    nodes = out_ref.shape[0]
    per = lanes // KGROUP
    at = pl.ds(pl.multiple_of(me_ref[0] * nodes, nodes), nodes)
    r = jnp.concatenate([ref[:, at] for ref in r_refs], axis=0)
    high = r.astype(BF16).astype(F32)
    parts = jnp.concatenate([high, r - high, high, r - high], axis=0).astype(BF16)
    rhs[...] = jnp.zeros(rhs.shape, BF16)
    for k in range(KGROUP):
        rhs[k * per : (k + 1) * per, k * nodes : (k + 1) * nodes] = parts

    wide = 512
    for b in range(0, nosc, step):
        best = None
        for n in range(0, rhs.shape[1], wide):
            for g in range(groups):
                history = jnp.abs(
                    jnp.dot(
                        t_ref[g, b : b + step, :], rhs[:, n : n + wide], preferred_element_type=F32
                    )
                )
                for k in range(0, wide, nodes):
                    one = history[:, k : k + nodes]
                    best = one if best is None else jnp.maximum(best, one)
        out_ref[:, b : b + step] = best.T


def exchange(x, axis, count, bit):
    return lax.ppermute(x, axis, [(i, i ^ bit) for i in range(count)])


def everyone(x, axis):
    count = lax.axis_size(axis)
    if count & (count - 1):
        return jnp.concatenate([x] + [exchange(x, axis, count, p) for p in range(1, count)], axis=0)
    bit = 1
    while bit < count:
        x = jnp.concatenate([x, exchange(x, axis, count, bit)], axis=0)
        bit *= 2
    return x


def on_device(
    load,
    a_tile,
    left_tile,
    right_tile,
    block_mask,
    left_blocks,
    right_blocks,
    motion,
    freq_values,
    node_dof,
    node_owner,
):
    m, cols = load.shape[2:]
    half = cols // 2
    face = left_tile.shape[-1]
    bs = m // NB
    nsub, fcount = lax.axis_size("sub"), lax.axis_size("freq")
    sub, freq = lax.axis_index("sub"), lax.axis_index("freq")
    nodes_sub = node_dof.shape[1]
    nodes_own = nodes_sub // fcount
    parity = (sub % 2).astype(jnp.int32)
    even = parity == 0

    def swap_pairs(x, start):
        pairs = []
        for i in range(start, nsub - 1, 2):
            pairs += [(i, i + 1), (i + 1, i)]
        return lax.ppermute(x, "sub", pairs)

    near = functools.partial(swap_pairs, start=0)
    far = functools.partial(swap_pairs, start=1)

    left_ids, right_ids = left_blocks[0], right_blocks[0]
    send_b = far(jnp.where(even, left_ids, right_ids))
    send_a = near(jnp.where(even, right_ids, left_ids))

    load_h, tile_h, left_h, right_h = hbm(load[0, 0], a_tile[0, 0], left_tile[0, 0], right_tile[0, 0])

    packed = pltpu.VMEM((face, cols), BF16)
    doubled = pltpu.VMEM((2 * m, cols), BF16)
    (v0,) = vmem(
        call(
            load_kernel,
            pltpu.VMEM((m, cols), F32),
            [HB],
            VM,
            [pltpu.SemaphoreType.DMA((6,))],
            limit=4,
        )(load_h)
    )
    count = left_ids.shape[0]
    rows_out = jax.ShapeDtypeStruct((face, cols), BF16)
    pack_a, pack_b = call(
        pack_kernel,
        (rows_out, rows_out),
        [SM, SM, VM],
        (HB, HB),
        [pltpu.VMEM((2, count, bs, cols), BF16), pltpu.SemaphoreType.DMA((2, count))],
        limit=4,
    )(send_a, send_b, v0)
    far1 = far(pack_b)
    near1 = near(pack_a)

    lanes = KGROUP * 8 * fcount
    me = freq.astype(jnp.int32).reshape(1)
    step = m // 3
    tile_shape, side = pltpu.VMEM((2, m, m), BF16), pltpu.VMEM((2, m, face), BF16)
    table, v0b, *tiles = call(
        functools.partial(table_kernel, fcount, step),
        (
            pltpu.VMEM((NT // KGROUP, NOSC, lanes), BF16),
            doubled,
            tile_shape,
            side,
            side,
        ),
        [SM, SM] + [HB] * 4 + [VM],
        (VM,) * 5,
        [pltpu.SemaphoreType.DMA((3, 2))],
        limit=6,
    )(freq_values, me, tile_h, left_h, right_h, pack_b, v0)

    mask = block_mask[0]
    parity1 = parity.reshape(1)
    image_shape = pltpu.VMEM((m, cols), F32)
    near_rhs = pltpu.VMEM((2 * face, cols), BF16)
    own1, tile, left, right = call(
        functools.partial(own_kernel, True, step),
        (image_shape, tile_shape, side, side),
        [SM, SM] + [HB] * 3 + [VM] * 5,
        (VM,) * 4,
        [near_rhs, pltpu.SemaphoreType.DMA((m // step - 1, 3, 2))],
        limit=10,
        aliases={5: 1, 6: 2, 7: 3},
    )(mask, parity1, tile_h, left_h, right_h, *vmem(*tiles, v0b, near1))
    tile, left, right = vmem(tile, left, right)

    rhs_scratch = pltpu.VMEM((2 * face, cols), BF16)
    pack_a2, pack_b2, token = call(
        faces_kernel,
        (packed, packed, jax.ShapeDtypeStruct((8, 128), F32)),
        [SM, SM, SM, VM, VM, VM, VM],
        (VM, VM, VM),
        [rhs_scratch, pltpu.VMEM((2 * face, 2 * face), BF16)],
        limit=8,
    )(send_a, send_b, parity1, *vmem(own1), left, right, *vmem(far1))
    far2 = far(pack_b2)
    near2 = near(pack_a2)
    v1, v1b = call(
        functools.partial(image_kernel, 512),
        (image_shape, doubled),
        [SM, VM, VM, VM, VM, HB],
        (VM, VM),
        [rhs_scratch],
        limit=8,
    )(parity1, *vmem(own1), left, right, *vmem(far1), token)
    (v1,) = vmem(v1)
    sums1 = call(
        functools.partial(sums_kernel, 128),
        jax.ShapeDtypeStruct((8, half), F32),
        [VM, VM],
        VM,
        limit=4,
    )(v0, v1)

    own2 = call(
        functools.partial(own_kernel, False, step),
        image_shape,
        [SM, SM] + [VM] * 5,
        VM,
        [near_rhs],
        limit=10,
    )(mask, parity1, tile, left, right, *vmem(v1b, near2))

    owner, dof = node_owner[0], node_dof[0]
    number = jnp.arange(nodes_sub, dtype=jnp.int32)
    before = (owner[:, None] == owner[None, :]) & (number[None, :] < number[:, None])
    slot = owner * nodes_own + jnp.sum(before.astype(jnp.int32), axis=1)
    dof_of = jnp.sum(jnp.where(slot[None, :] == number[:, None], dof[None, :], 0), axis=1)
    sums = call(
        functools.partial(second_kernel, 256),
        jax.ShapeDtypeStruct((8, half), F32),
        [SM] + [VM] * 7,
        VM,
        [rhs_scratch],
        limit=8,
    )(parity1, *vmem(own2), left, right, *vmem(far2), v0, v1, sums1)

    picks, bit = [], 1
    while bit < nsub or len(picks) < 2:
        got = exchange(sums, "sub", nsub, bit) if bit < nsub else jnp.zeros_like(sums)
        if bit > 1 and len(picks) < 2:
            rows, sums = call(
                functools.partial(pick_kernel, len(picks) * nodes_sub // 2),
                (
                    pltpu.VMEM((nodes_sub // 2, 2 * cols), F32),
                    jax.ShapeDtypeStruct((8, half), F32),
                ),
                [SM, VM, VM, VM],
                (VM, VM),
                limit=4,
            )(dof_of, v0, v1, sums)
            picks += vmem(rows)
        sums = sums + got
        bit *= 2

    resp, h = call(
        resp_kernel,
        (jax.ShapeDtypeStruct((2, nodes_sub), F32), jax.ShapeDtypeStruct((8, half), F32)),
        [VM, VM, VM, VM],
        (VM, VM),
        limit=4,
    )(sums, motion, *picks)
    arrived = everyone(resp, "freq")
    solution = call(
        sol_kernel,
        jax.ShapeDtypeStruct((m, cols), F32),
        [VM, VM, VM],
        HB,
        [pltpu.VMEM((m, cols), F32), pltpu.SemaphoreType.DMA((6,))],
        limit=6,
    )(h, v0, *vmem(v1))

    spectra = call(
        functools.partial(spec_kernel, 256),
        jax.ShapeDtypeStruct((nodes_own, NOSC), F32),
        [SM, VM, VM],
        VM,
        [pltpu.VMEM((lanes, KGROUP * nodes_own), BF16)],
        limit=8,
    )(me, arrived, *vmem(table))
    return solution[None, None], spectra[None]


def solution(mesh):
    placed = (
        P("sub", "freq", None, None),
        P("sub", "freq", None, None, None),
        P("sub", "freq", None, None, None),
        P("sub", "freq", None, None, None),
        P("sub", None, None),
        P("sub", None),
        P("sub", None),
        P("freq", None),
        P(),
        P("sub", None),
        P("sub", None),
    )
    return jax.shard_map(
        on_device,
        mesh=mesh,
        in_specs=placed,
        out_specs=(P("sub", "freq", None, None), P("sub", "freq", None)),
        check_vma=False,
    )
```

```python
import functools
import math

import jax
import jax.numpy as jnp
from jax import lax
from jax.experimental import pallas as pl
from jax.experimental.pallas import tpu as pltpu
from jax.sharding import PartitionSpec as P

NB = 12
NOSC = 1024
NT = 64
KGROUP = 8
EPSILON = 1e-06
DAMPING = 0.05
TIME_STEP = 0.01
MIB = 1024 * 1024

VM = pl.BlockSpec(memory_space=pltpu.VMEM)
SM = pl.BlockSpec(memory_space=pltpu.SMEM)
HB = pl.BlockSpec(memory_space=pl.ANY)
F32 = jnp.float32
BF16 = jnp.bfloat16


def hbm(*arrays):
    return [pltpu.with_memory_space_constraint(x, pltpu.HBM) for x in arrays]


def vmem(*arrays):
    return [pltpu.with_memory_space_constraint(x, pltpu.VMEM) for x in arrays]


def call(kernel, outs, in_specs, out_specs, scratch=(), limit=40, aliases=None):
    return pl.pallas_call(
        kernel,
        out_shape=outs,
        in_specs=in_specs,
        out_specs=out_specs,
        scratch_shapes=list(scratch),
        input_output_aliases=aliases or {},
        compiler_params=pltpu.CompilerParams(vmem_limit_bytes=limit * MIB),
    )


def turned(v):
    half = v.shape[-1] // 2
    return jnp.concatenate([-v[:, half:], v[:, :half]], axis=1)


def load_kernel(load_ref, v0_ref, sems):
    m = v0_ref.shape[0]
    chunks = sems.shape[0]
    size = m // chunks
    copies = []
    for c in range(chunks):
        rows = pl.ds(c * size, size)
        copies.append(pltpu.make_async_copy(load_ref.at[rows], v0_ref.at[rows], sems.at[c]))
    for copy in copies:
        copy.start()
    for copy in copies:
        copy.wait()


def pack_kernel(idb_ref, ida_ref, v0_ref, sa_ref, sb_ref, buf, sems):
    count = ida_ref.shape[0]
    rows = sa_ref.shape[0] // count
    copies = []
    for k, (ids, out) in enumerate(((idb_ref, sb_ref), (ida_ref, sa_ref))):
        for b in range(count):
            at = pl.ds(pl.multiple_of(ids[b] * rows, rows), rows)
            buf[k, b] = v0_ref[at].astype(BF16)
            copies.append(
                pltpu.make_async_copy(buf.at[k, b], out.at[pl.ds(b * rows, rows)], sems.at[k, b])
            )
            copies[-1].start()
    for copy in copies:
        copy.wait()


def own_kernel(first, step, mask_ref, par_ref, *rest):
    if first:
        sources, rest = rest[:3], rest[6:]
        v_ref, ra_ref, own_ref, a_ref, l_ref, r_ref, rhs, sems = rest
    else:
        a_ref, l_ref, r_ref, v_ref, ra_ref, own_ref, rhs = rest
    m, face = own_ref.shape[0], ra_ref.shape[0]
    bs = m // NB

    def fetch(i):
        rows = pl.ds(pl.multiple_of(i * step, step), step)
        return [
            pltpu.make_async_copy(source.at[c, rows], to.at[c, rows], sems.at[i - 1, k, c])
            for k, (source, to) in enumerate(zip(sources, (a_ref, l_ref, r_ref)))
            for c in range(2)
        ]

    if first:
        for i in range(1, m // step):
            for copy in fetch(i):
                copy.start()
    ra = ra_ref[...]
    rhs[0:face] = ra
    rhs[face:] = turned(ra)
    even = par_ref[0] == 0

    @pl.loop(0, m // step)
    def _(i):
        if first:

            @pl.when(i > 0)
            def _():
                for copy in fetch(i):
                    copy.wait()

        own, near = [], []
        for sub in range(step // bs):
            brow = i * (step // bs) + sub
            at = pl.ds(pl.multiple_of(i * step + sub * bs, bs), bs)
            keep = [(mask_ref[brow, j] != 0) | (brow == j) for j in range(NB)]
            pieces = []
            for c in range(2):
                for j in range(NB):
                    block = a_ref[c, at, j * bs : (j + 1) * bs]
                    pieces.append(lax.select(keep[j], block, jnp.zeros_like(block)))
            own.append(jnp.concatenate(pieces, axis=1))
            near.append(
                jnp.concatenate(
                    [lax.select(even, r_ref[c, at, :], l_ref[c, at, :]) for c in range(2)], axis=1
                )
            )
        rows = pl.ds(pl.multiple_of(i * step, step), step)
        out = jnp.dot(jnp.concatenate(own, axis=0), v_ref[...], preferred_element_type=F32)
        out += jnp.dot(jnp.concatenate(near, axis=0), rhs[...], preferred_element_type=F32)
        own_ref[rows, :] = out


def far_rhs(rb_ref, rhs):
    rb = rb_ref[...]
    face = rb.shape[0]
    rhs[0:face] = rb
    rhs[face:] = turned(rb)


def far_lhs(par_ref, l_ref, r_ref, rows):
    even = par_ref[0] == 0
    return jnp.concatenate(
        [lax.select(even, l_ref[c, rows, :], r_ref[c, rows, :]) for c in range(2)], axis=1
    )


def fold(x):
    return jnp.sum(x.reshape(x.shape[0] // 8, 8, x.shape[1]), axis=0)


def faces_kernel(ida_ref, idb_ref, par_ref, own_ref, l_ref, r_ref, rb_ref, *rest):
    sa_ref, sb_ref, token_ref, rhs, lhs = rest
    token_ref[...] = jnp.zeros(token_ref.shape, F32)
    count = ida_ref.shape[0]
    rows = sa_ref.shape[0] // count
    far_rhs(rb_ref, rhs)
    ats = [
        pl.ds(pl.multiple_of(ids[b] * rows, rows), rows)
        for ids in (idb_ref, ida_ref)
        for b in range(count)
    ]
    for k, at in enumerate(ats):
        lhs[k * rows : (k + 1) * rows] = far_lhs(par_ref, l_ref, r_ref, at)
    part = jnp.dot(lhs[...], rhs[...], preferred_element_type=F32)
    for k, at in enumerate(ats):
        out = (own_ref[at, :] + part[k * rows : (k + 1) * rows]).astype(BF16)
        to = (k % count) * rows
        (sb_ref if k < count else sa_ref)[to : to + rows] = out


def image_kernel(step, par_ref, own_ref, l_ref, r_ref, rb_ref, _, v1_ref, vb_ref, rhs):
    m = own_ref.shape[0]
    far_rhs(rb_ref, rhs)
    for i in range(m // step):
        rows = pl.ds(i * step, step)
        lhs = far_lhs(par_ref, l_ref, r_ref, rows)
        v1 = own_ref[rows, :] + jnp.dot(lhs, rhs[...], preferred_element_type=F32)
        v1_ref[rows, :] = v1
        vb = v1.astype(BF16)
        vb_ref[rows, :] = vb
        vb_ref[pl.ds(m + i * step, step), :] = turned(vb)


def sums_kernel(step, v0_ref, v1_ref, s_ref):
    m = v0_ref.shape[0]
    half = v0_ref.shape[1] // 2
    zero = jnp.zeros((8, half), F32)
    acc = (zero,) * 3
    for i in range(m // step):
        rows = pl.ds(i * step, step)
        ar, ai = v0_ref[rows, :half], v0_ref[rows, half:]
        br, bi = v1_ref[rows, :half], v1_ref[rows, half:]
        acc = (
            acc[0] + fold(br * ar + bi * ai),
            acc[1] + fold(br * ai - bi * ar),
            acc[2] + fold(br * br + bi * bi),
        )
    for k in range(3):
        s_ref[k : k + 1, :] = jnp.sum(acc[k], axis=0, keepdims=True)
    s_ref[3:, :] = jnp.zeros((5, half), F32)


def second_kernel(step, par_ref, own_ref, l_ref, r_ref, rb_ref, v0_ref, v1_ref, s1_ref, s_ref, rhs):
    m = own_ref.shape[0]
    half = v0_ref.shape[1] // 2
    far_rhs(rb_ref, rhs)

    zero = jnp.zeros((8, half), F32)
    acc = (zero,) * 5
    for i in range(m // step):
        rows = pl.ds(i * step, step)
        lhs = far_lhs(par_ref, l_ref, r_ref, rows)
        w = own_ref[rows, :] + jnp.dot(lhs, rhs[...], preferred_element_type=F32)
        ar, ai = v0_ref[rows, :half], v0_ref[rows, half:]
        br, bi = v1_ref[rows, :half], v1_ref[rows, half:]
        wr, wi = w[:, :half], w[:, half:]
        acc = (
            acc[0] + fold(wr * ar + wi * ai),
            acc[1] + fold(wr * ai - wi * ar),
            acc[2] + fold(wr * br + wi * bi),
            acc[3] + fold(wr * bi - wi * br),
            acc[4] + fold(wr * wr + wi * wi),
        )

    s_ref[...] = s1_ref[...]
    for k in range(5):
        s_ref[3 + k : 4 + k, :] = jnp.sum(acc[k], axis=0, keepdims=True)


def pick_kernel(first, dof_ref, v0_ref, v1_ref, s_ref, out_ref, again_ref):
    again_ref[...] = s_ref[...]
    cols = v0_ref.shape[1]

    @pl.loop(0, out_ref.shape[0] // 8)
    def _(g):
        base = pl.multiple_of(g * 8, 8)
        at = [dof_ref[first + base + r] for r in range(8)]
        for k, v_ref in enumerate((v0_ref, v1_ref)):
            out_ref[pl.ds(base, 8), k * cols : (k + 1) * cols] = jnp.concatenate(
                [v_ref[pl.ds(a, 1), :] for a in at], axis=0
            )


def cmul(x, y):
    return x[0] * y[0] - x[1] * y[1], x[0] * y[1] + x[1] * y[0]


def resp_kernel(s_ref, motion_ref, p0_ref, p1_ref, r_ref, h_ref):
    half = s_ref.shape[1]
    row = lambda k: s_ref[k : k + 1, :]
    cross1, energy1 = (row(0), row(1)), row(2)
    a1 = tuple(c / (energy1 + EPSILON) for c in cross1)
    conj = (a1[0], -a1[1])
    wv0, wv1, ww = (row(3), row(4)), (row(5), row(6)), row(7)
    size = a1[0] * a1[0] + a1[1] * a1[1]
    p0, p1 = cmul(conj, wv0), cmul(conj, wv1)
    cross2 = tuple(a1[k] * EPSILON - p0[k] + size * wv1[k] for k in range(2))
    energy2 = jnp.maximum(energy1 - 2.0 * p1[0] + size * ww, 0.0)
    a2 = tuple(c / (energy2 + EPSILON) for c in cross2)
    both = cmul(a1, a2)
    h0 = (a1[0] + a2[0], a1[1] + a2[1])
    h1 = (-both[0], -both[1])
    h_ref[0:1], h_ref[1:2], h_ref[2:3], h_ref[3:4] = h0[0], h0[1], h1[0], h1[1]
    h_ref[4:] = jnp.zeros((4, half), F32)
    mo = (motion_ref[0:1, :half], motion_ref[0:1, half:])
    g0, g1 = cmul(h0, mo), cmul(h1, mo)
    chunk = 128
    part = p0_ref.shape[0] // chunk
    for i in range(2 * part):
        pick_ref = p0_ref if i < part else p1_ref
        rows = slice(i % part * chunk, (i % part + 1) * chunk)
        to = slice(i * chunk, (i + 1) * chunk)
        re = im = None
        for t in range(half // 128):
            at = slice(t * 128, (t + 1) * 128)
            x = [pick_ref[rows, k * half + t * 128 : k * half + (t + 1) * 128] for k in range(4)]
            c = [g[:, at] for g in (*g0, *g1)]
            one = c[0] * x[0] - c[1] * x[1] + c[2] * x[2] - c[3] * x[3]
            two = c[0] * x[1] + c[1] * x[0] + c[2] * x[3] + c[3] * x[2]
            re = one if re is None else re + one
            im = two if im is None else im + two
        r_ref[0:1, to] = jnp.sum(re.T, axis=0, keepdims=True)
        r_ref[1:2, to] = jnp.sum(im.T, axis=0, keepdims=True)


def sol_kernel(h_ref, v0_ref, v1_ref, out_ref, buf, sems):
    chunks = sems.shape[0]
    half = h_ref.shape[1]
    rows = buf.shape[0] // chunks
    h = [h_ref[k : k + 1, :] for k in range(4)]
    for c in range(chunks):
        at = slice(c * rows, (c + 1) * rows)
        ar, ai = v0_ref[at, :half], v0_ref[at, half:]
        br, bi = v1_ref[at, :half], v1_ref[at, half:]
        buf[at, :half] = h[0] * ar - h[1] * ai + h[2] * br - h[3] * bi
        buf[at, half:] = h[0] * ai + h[1] * ar + h[2] * bi + h[3] * br
        pltpu.make_async_copy(
            buf.at[pl.ds(c * rows, rows)], out_ref.at[pl.ds(c * rows, rows)], sems.at[c]
        ).start()
    for c in range(chunks):
        pltpu.make_async_copy(
            buf.at[pl.ds(c * rows, rows)], out_ref.at[pl.ds(c * rows, rows)], sems.at[c]
        ).wait()


def table_kernel(fcount, first, f_ref, me_ref, *rest):
    sources, v0_ref, out_ref, vb_ref, tiles, sems = rest[:3], rest[4], *rest[5:7], rest[7:10], rest[10]
    copies = []
    for k in range(3):
        for c in range(2):
            rows = pl.ds(0, first)
            copies.append(
                pltpu.make_async_copy(
                    sources[k].at[c, rows], tiles[k].at[c, rows], sems.at[k, c]
                )
            )
    for copy in copies:
        copy.start()
    groups, nosc, lanes = out_ref.shape
    step = 128
    lane = lax.broadcasted_iota(jnp.int32, (groups, lanes), 1)
    of = (lane % (2 * fcount)) // 2
    wls = jnp.zeros((groups, lanes), F32)
    for p in range(fcount):
        wls = jnp.where(of == p, 2.0 * math.pi * f_ref[me_ref[0] ^ p], wls)
    number = lax.broadcasted_iota(jnp.int32, (groups, lanes), 0) * KGROUP + lane // (8 * fcount)
    phase = wls * (number.astype(F32) * TIME_STEP)
    cosine, sine = jnp.cos(phase), jnp.sin(phase)
    real = lane % 2 == 0
    xs, ys = jnp.where(real, cosine, -sine), jnp.where(real, -sine, -cosine)
    wl = wls[0:1]
    low = (lax.broadcasted_iota(jnp.int32, (step, lanes), 1) // (2 * fcount)) % 4 >= 2

    @pl.loop(0, nosc // step)
    def _(b):
        rows = pl.ds(pl.multiple_of(b * step, step), step)
        index = (lax.broadcasted_iota(jnp.int32, (step, lanes), 0) + b * step).astype(F32)
        osc = (2.0 * math.pi * 0.5) * jnp.exp(index * (math.log(100.0) / (nosc - 1)))
        stiffness = osc * osc
        damping = 2.0 * DAMPING * osc * wl
        detuning = stiffness - wl * wl
        scale = 1.0 / ((detuning * detuning + damping * damping) * fcount)
        gr = (stiffness * detuning + damping * damping) * scale
        gi = (damping * detuning - stiffness * damping) * scale
        for k in range(groups):
            value = xs[k : k + 1] * gr + ys[k : k + 1] * gi
            high = value.astype(BF16).astype(F32)
            out_ref[k, rows, :] = jnp.where(low, value - high, high).astype(BF16)

    m = v0_ref.shape[0]
    vb = v0_ref[...].astype(BF16)
    vb_ref[0:m] = vb
    vb_ref[m:] = turned(vb)
    for copy in copies:
        copy.wait()


def spec_kernel(step, me_ref, *rest):
    r_refs, (t_ref, out_ref, rhs) = rest[:-3], rest[-3:]
    groups, nosc, lanes = t_ref.shape
    nodes = out_ref.shape[0]
    per = lanes // KGROUP
    at = pl.ds(pl.multiple_of(me_ref[0] * nodes, nodes), nodes)
    r = jnp.concatenate([ref[:, at] for ref in r_refs], axis=0)
    high = r.astype(BF16).astype(F32)
    parts = jnp.concatenate([high, r - high, high, r - high], axis=0).astype(BF16)
    rhs[...] = jnp.zeros(rhs.shape, BF16)
    for k in range(KGROUP):
        rhs[k * per : (k + 1) * per, k * nodes : (k + 1) * nodes] = parts

    wide = 512
    for b in range(0, nosc, step):
        best = None
        for n in range(0, rhs.shape[1], wide):
            for g in range(groups):
                history = jnp.abs(
                    jnp.dot(
                        t_ref[g, b : b + step, :], rhs[:, n : n + wide], preferred_element_type=F32
                    )
                )
                for k in range(0, wide, nodes):
                    one = history[:, k : k + nodes]
                    best = one if best is None else jnp.maximum(best, one)
        out_ref[:, b : b + step] = best.T


def exchange(x, axis, count, bit):
    return lax.ppermute(x, axis, [(i, i ^ bit) for i in range(count)])


def everyone(x, axis):
    count = lax.axis_size(axis)
    if count & (count - 1):
        return jnp.concatenate([x] + [exchange(x, axis, count, p) for p in range(1, count)], axis=0)
    bit = 1
    while bit < count:
        x = jnp.concatenate([x, exchange(x, axis, count, bit)], axis=0)
        bit *= 2
    return x


def on_device(
    load,
    a_tile,
    left_tile,
    right_tile,
    block_mask,
    left_blocks,
    right_blocks,
    motion,
    freq_values,
    node_dof,
    node_owner,
):
    m, cols = load.shape[2:]
    half = cols // 2
    face = left_tile.shape[-1]
    bs = m // NB
    nsub, fcount = lax.axis_size("sub"), lax.axis_size("freq")
    sub, freq = lax.axis_index("sub"), lax.axis_index("freq")
    nodes_sub = node_dof.shape[1]
    nodes_own = nodes_sub // fcount
    parity = (sub % 2).astype(jnp.int32)
    even = parity == 0

    def swap_pairs(x, start):
        pairs = []
        for i in range(start, nsub - 1, 2):
            pairs += [(i, i + 1), (i + 1, i)]
        return lax.ppermute(x, "sub", pairs)

    near = functools.partial(swap_pairs, start=0)
    far = functools.partial(swap_pairs, start=1)

    left_ids, right_ids = left_blocks[0], right_blocks[0]
    send_b = far(jnp.where(even, left_ids, right_ids))
    send_a = near(jnp.where(even, right_ids, left_ids))

    load_h, tile_h, left_h, right_h = hbm(load[0, 0], a_tile[0, 0], left_tile[0, 0], right_tile[0, 0])

    packed = pltpu.VMEM((face, cols), BF16)
    doubled = pltpu.VMEM((2 * m, cols), BF16)
    (v0,) = vmem(
        call(
            load_kernel,
            pltpu.VMEM((m, cols), F32),
            [HB],
            VM,
            [pltpu.SemaphoreType.DMA((6,))],
            limit=4,
        )(load_h)
    )
    count = left_ids.shape[0]
    rows_out = jax.ShapeDtypeStruct((face, cols), BF16)
    pack_a, pack_b = call(
        pack_kernel,
        (rows_out, rows_out),
        [SM, SM, VM],
        (HB, HB),
        [pltpu.VMEM((2, count, bs, cols), BF16), pltpu.SemaphoreType.DMA((2, count))],
        limit=4,
    )(send_b, send_a, v0)
    far1 = far(pack_b)
    near1 = near(pack_a)

    lanes = KGROUP * 8 * fcount
    me = freq.astype(jnp.int32).reshape(1)
    step = m // 3
    tile_shape, side = pltpu.VMEM((2, m, m), BF16), pltpu.VMEM((2, m, face), BF16)
    table, v0b, *tiles = call(
        functools.partial(table_kernel, fcount, step),
        (
            pltpu.VMEM((NT // KGROUP, NOSC, lanes), BF16),
            doubled,
            tile_shape,
            side,
            side,
        ),
        [SM, SM] + [HB] * 4 + [VM],
        (VM,) * 5,
        [pltpu.SemaphoreType.DMA((3, 2))],
        limit=6,
    )(freq_values, me, tile_h, left_h, right_h, pack_b, v0)

    mask = block_mask[0]
    parity1 = parity.reshape(1)
    image_shape = pltpu.VMEM((m, cols), F32)
    near_rhs = pltpu.VMEM((2 * face, cols), BF16)
    own1, tile, left, right = call(
        functools.partial(own_kernel, True, step),
        (image_shape, tile_shape, side, side),
        [SM, SM] + [HB] * 3 + [VM] * 5,
        (VM,) * 4,
        [near_rhs, pltpu.SemaphoreType.DMA((m // step - 1, 3, 2))],
        limit=10,
        aliases={5: 1, 6: 2, 7: 3},
    )(mask, parity1, tile_h, left_h, right_h, *vmem(*tiles, v0b, near1))
    tile, left, right = vmem(tile, left, right)

    rhs_scratch = pltpu.VMEM((2 * face, cols), BF16)
    pack_a2, pack_b2, token = call(
        faces_kernel,
        (packed, packed, jax.ShapeDtypeStruct((8, 128), F32)),
        [SM, SM, SM, VM, VM, VM, VM],
        (VM, VM, VM),
        [rhs_scratch, pltpu.VMEM((2 * face, 2 * face), BF16)],
        limit=8,
    )(send_a, send_b, parity1, *vmem(own1), left, right, *vmem(far1))
    far2 = far(pack_b2)
    near2 = near(pack_a2)
    v1, v1b = call(
        functools.partial(image_kernel, 512),
        (image_shape, doubled),
        [SM, VM, VM, VM, VM, HB],
        (VM, VM),
        [rhs_scratch],
        limit=8,
    )(parity1, *vmem(own1), left, right, *vmem(far1), token)
    (v1,) = vmem(v1)
    sums1 = call(
        functools.partial(sums_kernel, 128),
        jax.ShapeDtypeStruct((8, half), F32),
        [VM, VM],
        VM,
        limit=4,
    )(v0, v1)

    own2 = call(
        functools.partial(own_kernel, False, step),
        image_shape,
        [SM, SM] + [VM] * 5,
        VM,
        [near_rhs],
        limit=10,
    )(mask, parity1, tile, left, right, *vmem(v1b, near2))

    owner, dof = node_owner[0], node_dof[0]
    number = jnp.arange(nodes_sub, dtype=jnp.int32)
    before = (owner[:, None] == owner[None, :]) & (number[None, :] < number[:, None])
    slot = owner * nodes_own + jnp.sum(before.astype(jnp.int32), axis=1)
    dof_of = jnp.sum(jnp.where(slot[None, :] == number[:, None], dof[None, :], 0), axis=1)
    sums = call(
        functools.partial(second_kernel, 256),
        jax.ShapeDtypeStruct((8, half), F32),
        [SM] + [VM] * 7,
        VM,
        [rhs_scratch],
        limit=8,
    )(parity1, *vmem(own2), left, right, *vmem(far2), v0, v1, sums1)

    picks, bit = [], 1
    while bit < nsub or len(picks) < 2:
        got = exchange(sums, "sub", nsub, bit) if bit < nsub else jnp.zeros_like(sums)
        if bit > 1 and len(picks) < 2:
            rows, sums = call(
                functools.partial(pick_kernel, len(picks) * nodes_sub // 2),
                (
                    pltpu.VMEM((nodes_sub // 2, 2 * cols), F32),
                    jax.ShapeDtypeStruct((8, half), F32),
                ),
                [SM, VM, VM, VM],
                (VM, VM),
                limit=4,
            )(dof_of, v0, v1, sums)
            picks += vmem(rows)
        sums = sums + got
        bit *= 2

    resp, h = call(
        resp_kernel,
        (jax.ShapeDtypeStruct((2, nodes_sub), F32), jax.ShapeDtypeStruct((8, half), F32)),
        [VM, VM, VM, VM],
        (VM, VM),
        limit=4,
    )(sums, motion, *picks)
    arrived = everyone(resp, "freq")
    solution = call(
        sol_kernel,
        jax.ShapeDtypeStruct((m, cols), F32),
        [VM, VM, VM],
        HB,
        [pltpu.VMEM((m, cols), F32), pltpu.SemaphoreType.DMA((6,))],
        limit=6,
    )(h, v0, *vmem(v1))

    spectra = call(
        functools.partial(spec_kernel, 256),
        jax.ShapeDtypeStruct((nodes_own, NOSC), F32),
        [SM, VM, VM],
        VM,
        [pltpu.VMEM((lanes, KGROUP * nodes_own), BF16)],
        limit=8,
    )(me, arrived, *vmem(table))
    return solution[None, None], spectra[None]


def solution(mesh):
    placed = (
        P("sub", "freq", None, None),
        P("sub", "freq", None, None, None),
        P("sub", "freq", None, None, None),
        P("sub", "freq", None, None, None),
        P("sub", None, None),
        P("sub", None),
        P("sub", None),
        P("freq", None),
        P(),
        P("sub", None),
        P("sub", None),
    )
    return jax.shard_map(
        on_device,
        mesh=mesh,
        in_specs=placed,
        out_specs=(P("sub", "freq", None, None), P("sub", "freq", None)),
        check_vma=False,
    )
```

```python
import functools
import math

import jax
import jax.numpy as jnp
from jax import lax
from jax.experimental import pallas as pl
from jax.experimental.pallas import tpu as pltpu
from jax.sharding import PartitionSpec as P

NB = 12
NOSC = 1024
NT = 64
KGROUP = 8
EPSILON = 1e-06
DAMPING = 0.05
TIME_STEP = 0.01
MIB = 1024 * 1024

VM = pl.BlockSpec(memory_space=pltpu.VMEM)
SM = pl.BlockSpec(memory_space=pltpu.SMEM)
HB = pl.BlockSpec(memory_space=pl.ANY)
F32 = jnp.float32
BF16 = jnp.bfloat16


def hbm(*arrays):
    return [pltpu.with_memory_space_constraint(x, pltpu.HBM) for x in arrays]


def vmem(*arrays):
    return [pltpu.with_memory_space_constraint(x, pltpu.VMEM) for x in arrays]


def call(kernel, outs, in_specs, out_specs, scratch=(), limit=40, aliases=None):
    return pl.pallas_call(
        kernel,
        out_shape=outs,
        in_specs=in_specs,
        out_specs=out_specs,
        scratch_shapes=list(scratch),
        input_output_aliases=aliases or {},
        compiler_params=pltpu.CompilerParams(vmem_limit_bytes=limit * MIB),
    )


def turned(v):
    half = v.shape[-1] // 2
    return jnp.concatenate([-v[:, half:], v[:, :half]], axis=1)


def load_kernel(load_ref, v0_ref, sems):
    m = v0_ref.shape[0]
    chunks = sems.shape[0]
    size = m // chunks
    copies = []
    for c in range(chunks):
        rows = pl.ds(c * size, size)
        copies.append(pltpu.make_async_copy(load_ref.at[rows], v0_ref.at[rows], sems.at[c]))
    for copy in copies:
        copy.start()
    for copy in copies:
        copy.wait()


def pack_kernel(idb_ref, ida_ref, v0_ref, sa_ref, sb_ref, buf, sems):
    count = ida_ref.shape[0]
    rows = sa_ref.shape[0] // count
    copies = []
    for k, (ids, out) in enumerate(((idb_ref, sb_ref), (ida_ref, sa_ref))):
        for b in range(count):
            at = pl.ds(pl.multiple_of(ids[b] * rows, rows), rows)
            buf[k, b] = v0_ref[at].astype(BF16)
            copies.append(
                pltpu.make_async_copy(buf.at[k, b], out.at[pl.ds(b * rows, rows)], sems.at[k, b])
            )
            copies[-1].start()
    for copy in copies:
        copy.wait()


def own_kernel(first, step, mask_ref, par_ref, *rest):
    if first:
        sources, rest = rest[:3], rest[6:]
        v_ref, ra_ref, own_ref, a_ref, l_ref, r_ref, rhs, sems = rest
    else:
        a_ref, l_ref, r_ref, v_ref, ra_ref, own_ref, rhs = rest
    m, face = own_ref.shape[0], ra_ref.shape[0]
    bs = m // NB

    def fetch(i):
        rows = pl.ds(pl.multiple_of(i * step, step), step)
        return [
            pltpu.make_async_copy(source.at[c, rows], to.at[c, rows], sems.at[i - 1, k, c])
            for k, (source, to) in enumerate(zip(sources, (a_ref, l_ref, r_ref)))
            for c in range(2)
        ]

    if first:
        for i in range(1, m // step):
            for copy in fetch(i):
                copy.start()
    ra = ra_ref[...]
    rhs[0:face] = ra
    rhs[face:] = turned(ra)
    even = par_ref[0] == 0

    @pl.loop(0, m // step)
    def _(i):
        if first:

            @pl.when(i > 0)
            def _():
                for copy in fetch(i):
                    copy.wait()

        own, near = [], []
        for sub in range(step // bs):
            brow = i * (step // bs) + sub
            at = pl.ds(pl.multiple_of(i * step + sub * bs, bs), bs)
            keep = [(mask_ref[brow, j] != 0) | (brow == j) for j in range(NB)]
            pieces = []
            for c in range(2):
                for j in range(NB):
                    block = a_ref[c, at, j * bs : (j + 1) * bs]
                    pieces.append(lax.select(keep[j], block, jnp.zeros_like(block)))
            own.append(jnp.concatenate(pieces, axis=1))
            near.append(
                jnp.concatenate(
                    [lax.select(even, r_ref[c, at, :], l_ref[c, at, :]) for c in range(2)], axis=1
                )
            )
        rows = pl.ds(pl.multiple_of(i * step, step), step)
        out = jnp.dot(jnp.concatenate(own, axis=0), v_ref[...], preferred_element_type=F32)
        out += jnp.dot(jnp.concatenate(near, axis=0), rhs[...], preferred_element_type=F32)
        own_ref[rows, :] = out


def far_rhs(rb_ref, rhs):
    rb = rb_ref[...]
    face = rb.shape[0]
    rhs[0:face] = rb
    rhs[face:] = turned(rb)


def far_lhs(par_ref, l_ref, r_ref, rows):
    even = par_ref[0] == 0
    return jnp.concatenate(
        [lax.select(even, l_ref[c, rows, :], r_ref[c, rows, :]) for c in range(2)], axis=1
    )


def fold(x):
    return jnp.sum(x.reshape(x.shape[0] // 8, 8, x.shape[1]), axis=0)


def faces_kernel(ida_ref, idb_ref, par_ref, own_ref, l_ref, r_ref, rb_ref, *rest):
    sa_ref, sb_ref, token_ref, rhs, lhs = rest
    token_ref[...] = jnp.zeros(token_ref.shape, F32)
    count = ida_ref.shape[0]
    rows = sa_ref.shape[0] // count
    far_rhs(rb_ref, rhs)
    ats = [
        pl.ds(pl.multiple_of(ids[b] * rows, rows), rows)
        for ids in (idb_ref, ida_ref)
        for b in range(count)
    ]
    for k, at in enumerate(ats):
        lhs[k * rows : (k + 1) * rows] = far_lhs(par_ref, l_ref, r_ref, at)
    part = jnp.dot(lhs[...], rhs[...], preferred_element_type=F32)
    for k, at in enumerate(ats):
        out = (own_ref[at, :] + part[k * rows : (k + 1) * rows]).astype(BF16)
        to = (k % count) * rows
        (sb_ref if k < count else sa_ref)[to : to + rows] = out


def image_kernel(step, par_ref, own_ref, l_ref, r_ref, rb_ref, _, v1_ref, vb_ref, rhs):
    m = own_ref.shape[0]
    far_rhs(rb_ref, rhs)
    for i in range(m // step):
        rows = pl.ds(i * step, step)
        lhs = far_lhs(par_ref, l_ref, r_ref, rows)
        v1 = own_ref[rows, :] + jnp.dot(lhs, rhs[...], preferred_element_type=F32)
        v1_ref[rows, :] = v1
        vb = v1.astype(BF16)
        vb_ref[rows, :] = vb
        vb_ref[pl.ds(m + i * step, step), :] = turned(vb)


def sums_kernel(step, v0_ref, v1_ref, s_ref):
    m = v0_ref.shape[0]
    half = v0_ref.shape[1] // 2
    zero = jnp.zeros((8, half), F32)
    acc = (zero,) * 3
    for i in range(m // step):
        rows = pl.ds(i * step, step)
        ar, ai = v0_ref[rows, :half], v0_ref[rows, half:]
        br, bi = v1_ref[rows, :half], v1_ref[rows, half:]
        acc = (
            acc[0] + fold(br * ar + bi * ai),
            acc[1] + fold(br * ai - bi * ar),
            acc[2] + fold(br * br + bi * bi),
        )
    for k in range(3):
        s_ref[k : k + 1, :] = jnp.sum(acc[k], axis=0, keepdims=True)
    s_ref[3:, :] = jnp.zeros((5, half), F32)


def second_kernel(step, par_ref, own_ref, l_ref, r_ref, rb_ref, v0_ref, v1_ref, s1_ref, s_ref, rhs):
    m = own_ref.shape[0]
    half = v0_ref.shape[1] // 2
    far_rhs(rb_ref, rhs)

    zero = jnp.zeros((8, half), F32)
    acc = (zero,) * 5
    for i in range(m // step):
        rows = pl.ds(i * step, step)
        lhs = far_lhs(par_ref, l_ref, r_ref, rows)
        w = own_ref[rows, :] + jnp.dot(lhs, rhs[...], preferred_element_type=F32)
        ar, ai = v0_ref[rows, :half], v0_ref[rows, half:]
        br, bi = v1_ref[rows, :half], v1_ref[rows, half:]
        wr, wi = w[:, :half], w[:, half:]
        acc = (
            acc[0] + fold(wr * ar + wi * ai),
            acc[1] + fold(wr * ai - wi * ar),
            acc[2] + fold(wr * br + wi * bi),
            acc[3] + fold(wr * bi - wi * br),
            acc[4] + fold(wr * wr + wi * wi),
        )

    s_ref[...] = s1_ref[...]
    for k in range(5):
        s_ref[3 + k : 4 + k, :] = jnp.sum(acc[k], axis=0, keepdims=True)


def pick_kernel(first, dof_ref, v0_ref, v1_ref, s_ref, out_ref, again_ref):
    again_ref[...] = s_ref[...]
    cols = v0_ref.shape[1]

    @pl.loop(0, out_ref.shape[0] // 8)
    def _(g):
        base = pl.multiple_of(g * 8, 8)
        at = [dof_ref[first + base + r] for r in range(8)]
        for k, v_ref in enumerate((v0_ref, v1_ref)):
            out_ref[pl.ds(base, 8), k * cols : (k + 1) * cols] = jnp.concatenate(
                [v_ref[pl.ds(a, 1), :] for a in at], axis=0
            )


def cmul(x, y):
    return x[0] * y[0] - x[1] * y[1], x[0] * y[1] + x[1] * y[0]


def resp_kernel(s_ref, motion_ref, p0_ref, p1_ref, r_ref, h_ref):
    half = s_ref.shape[1]
    row = lambda k: s_ref[k : k + 1, :]
    cross1, energy1 = (row(0), row(1)), row(2)
    a1 = tuple(c / (energy1 + EPSILON) for c in cross1)
    conj = (a1[0], -a1[1])
    wv0, wv1, ww = (row(3), row(4)), (row(5), row(6)), row(7)
    size = a1[0] * a1[0] + a1[1] * a1[1]
    p0, p1 = cmul(conj, wv0), cmul(conj, wv1)
    cross2 = tuple(a1[k] * EPSILON - p0[k] + size * wv1[k] for k in range(2))
    energy2 = jnp.maximum(energy1 - 2.0 * p1[0] + size * ww, 0.0)
    a2 = tuple(c / (energy2 + EPSILON) for c in cross2)
    both = cmul(a1, a2)
    h0 = (a1[0] + a2[0], a1[1] + a2[1])
    h1 = (-both[0], -both[1])
    h_ref[0:1], h_ref[1:2], h_ref[2:3], h_ref[3:4] = h0[0], h0[1], h1[0], h1[1]
    h_ref[4:] = jnp.zeros((4, half), F32)
    mo = (motion_ref[0:1, :half], motion_ref[0:1, half:])
    g0, g1 = cmul(h0, mo), cmul(h1, mo)
    chunk = 128
    part = p0_ref.shape[0] // chunk
    for i in range(2 * part):
        pick_ref = p0_ref if i < part else p1_ref
        rows = slice(i % part * chunk, (i % part + 1) * chunk)
        to = slice(i * chunk, (i + 1) * chunk)
        re = im = None
        for t in range(half // 128):
            at = slice(t * 128, (t + 1) * 128)
            x = [pick_ref[rows, k * half + t * 128 : k * half + (t + 1) * 128] for k in range(4)]
            c = [g[:, at] for g in (*g0, *g1)]
            one = c[0] * x[0] - c[1] * x[1] + c[2] * x[2] - c[3] * x[3]
            two = c[0] * x[1] + c[1] * x[0] + c[2] * x[3] + c[3] * x[2]
            re = one if re is None else re + one
            im = two if im is None else im + two
        r_ref[0:1, to] = jnp.sum(re.T, axis=0, keepdims=True)
        r_ref[1:2, to] = jnp.sum(im.T, axis=0, keepdims=True)


def sol_kernel(h_ref, v0_ref, v1_ref, out_ref, buf, sems):
    chunks = sems.shape[0]
    half = h_ref.shape[1]
    rows = buf.shape[0] // chunks
    h = [h_ref[k : k + 1, :] for k in range(4)]
    for c in range(chunks):
        at = slice(c * rows, (c + 1) * rows)
        ar, ai = v0_ref[at, :half], v0_ref[at, half:]
        br, bi = v1_ref[at, :half], v1_ref[at, half:]
        buf[at, :half] = h[0] * ar - h[1] * ai + h[2] * br - h[3] * bi
        buf[at, half:] = h[0] * ai + h[1] * ar + h[2] * bi + h[3] * br
        pltpu.make_async_copy(
            buf.at[pl.ds(c * rows, rows)], out_ref.at[pl.ds(c * rows, rows)], sems.at[c]
        ).start()
    for c in range(chunks):
        pltpu.make_async_copy(
            buf.at[pl.ds(c * rows, rows)], out_ref.at[pl.ds(c * rows, rows)], sems.at[c]
        ).wait()


def table_kernel(fcount, first, f_ref, me_ref, *rest):
    sources, v0_ref, out_ref, vb_ref, tiles, sems = rest[:3], rest[4], *rest[5:7], rest[7:10], rest[10]
    copies = []
    for k in range(3):
        for c in range(2):
            rows = pl.ds(0, first)
            copies.append(
                pltpu.make_async_copy(
                    sources[k].at[c, rows], tiles[k].at[c, rows], sems.at[k, c]
                )
            )
    for copy in copies:
        copy.start()
    groups, nosc, lanes = out_ref.shape
    step = 128
    lane = lax.broadcasted_iota(jnp.int32, (groups, lanes), 1)
    of = (lane % (2 * fcount)) // 2
    wls = jnp.zeros((groups, lanes), F32)
    for p in range(fcount):
        wls = jnp.where(of == p, 2.0 * math.pi * f_ref[me_ref[0] ^ p], wls)
    number = lax.broadcasted_iota(jnp.int32, (groups, lanes), 0) * KGROUP + lane // (8 * fcount)
    phase = wls * (number.astype(F32) * TIME_STEP)
    cosine, sine = jnp.cos(phase), jnp.sin(phase)
    real = lane % 2 == 0
    xs, ys = jnp.where(real, cosine, -sine), jnp.where(real, -sine, -cosine)
    wl = wls[0:1]
    low = (lax.broadcasted_iota(jnp.int32, (step, lanes), 1) // (2 * fcount)) % 4 >= 2

    @pl.loop(0, nosc // step)
    def _(b):
        rows = pl.ds(pl.multiple_of(b * step, step), step)
        index = (lax.broadcasted_iota(jnp.int32, (step, lanes), 0) + b * step).astype(F32)
        osc = (2.0 * math.pi * 0.5) * jnp.exp(index * (math.log(100.0) / (nosc - 1)))
        stiffness = osc * osc
        damping = 2.0 * DAMPING * osc * wl
        detuning = stiffness - wl * wl
        scale = 1.0 / ((detuning * detuning + damping * damping) * fcount)
        gr = (stiffness * detuning + damping * damping) * scale
        gi = (damping * detuning - stiffness * damping) * scale
        for k in range(groups):
            value = xs[k : k + 1] * gr + ys[k : k + 1] * gi
            high = value.astype(BF16).astype(F32)
            out_ref[k, rows, :] = jnp.where(low, value - high, high).astype(BF16)

    m = v0_ref.shape[0]
    vb = v0_ref[...].astype(BF16)
    vb_ref[0:m] = vb
    vb_ref[m:] = turned(vb)
    for copy in copies:
        copy.wait()


def spec_kernel(step, me_ref, *rest):
    r_refs, (t_ref, out_ref, rhs, buf, sems) = rest[:-5], rest[-5:]
    groups, nosc, lanes = t_ref.shape
    nodes = out_ref.shape[0]
    per = lanes // KGROUP
    at = pl.ds(pl.multiple_of(me_ref[0] * nodes, nodes), nodes)
    r = jnp.concatenate([ref[:, at] for ref in r_refs], axis=0)
    high = r.astype(BF16).astype(F32)
    parts = jnp.concatenate([high, r - high, high, r - high], axis=0).astype(BF16)
    rhs[...] = jnp.zeros(rhs.shape, BF16)
    for k in range(KGROUP):
        rhs[k * per : (k + 1) * per, k * nodes : (k + 1) * nodes] = parts

    wide, copies = 512, []
    for b in range(0, nosc, step):
        best = None
        for n in range(0, rhs.shape[1], wide):
            for g in range(groups):
                history = jnp.abs(
                    jnp.dot(
                        t_ref[g, b : b + step, :], rhs[:, n : n + wide], preferred_element_type=F32
                    )
                )
                for k in range(0, wide, nodes):
                    one = history[:, k : k + nodes]
                    best = one if best is None else jnp.maximum(best, one)
        buf[:, b : b + step] = best.T
        cols = pl.ds(b, step)
        copies.append(
            pltpu.make_async_copy(buf.at[:, cols], out_ref.at[:, cols], sems.at[b // step])
        )
        copies[-1].start()
    for copy in copies:
        copy.wait()


def exchange(x, axis, count, bit):
    return lax.ppermute(x, axis, [(i, i ^ bit) for i in range(count)])


def everyone(x, axis):
    count = lax.axis_size(axis)
    if count & (count - 1):
        return jnp.concatenate([x] + [exchange(x, axis, count, p) for p in range(1, count)], axis=0)
    bit = 1
    while bit < count:
        x = jnp.concatenate([x, exchange(x, axis, count, bit)], axis=0)
        bit *= 2
    return x


def on_device(
    load,
    a_tile,
    left_tile,
    right_tile,
    block_mask,
    left_blocks,
    right_blocks,
    motion,
    freq_values,
    node_dof,
    node_owner,
):
    m, cols = load.shape[2:]
    half = cols // 2
    face = left_tile.shape[-1]
    bs = m // NB
    nsub, fcount = lax.axis_size("sub"), lax.axis_size("freq")
    sub, freq = lax.axis_index("sub"), lax.axis_index("freq")
    nodes_sub = node_dof.shape[1]
    nodes_own = nodes_sub // fcount
    parity = (sub % 2).astype(jnp.int32)
    even = parity == 0

    def swap_pairs(x, start):
        pairs = []
        for i in range(start, nsub - 1, 2):
            pairs += [(i, i + 1), (i + 1, i)]
        return lax.ppermute(x, "sub", pairs)

    near = functools.partial(swap_pairs, start=0)
    far = functools.partial(swap_pairs, start=1)

    left_ids, right_ids = left_blocks[0], right_blocks[0]
    send_b = far(jnp.where(even, left_ids, right_ids))
    send_a = near(jnp.where(even, right_ids, left_ids))

    load_h, tile_h, left_h, right_h = hbm(load[0, 0], a_tile[0, 0], left_tile[0, 0], right_tile[0, 0])

    packed = pltpu.VMEM((face, cols), BF16)
    doubled = pltpu.VMEM((2 * m, cols), BF16)
    (v0,) = vmem(
        call(
            load_kernel,
            pltpu.VMEM((m, cols), F32),
            [HB],
            VM,
            [pltpu.SemaphoreType.DMA((6,))],
            limit=4,
        )(load_h)
    )
    count = left_ids.shape[0]
    rows_out = jax.ShapeDtypeStruct((face, cols), BF16)
    pack_a, pack_b = call(
        pack_kernel,
        (rows_out, rows_out),
        [SM, SM, VM],
        (HB, HB),
        [pltpu.VMEM((2, count, bs, cols), BF16), pltpu.SemaphoreType.DMA((2, count))],
        limit=4,
    )(send_b, send_a, v0)
    far1 = far(pack_b)
    near1 = near(pack_a)

    lanes = KGROUP * 8 * fcount
    me = freq.astype(jnp.int32).reshape(1)
    step = m // 3
    tile_shape, side = pltpu.VMEM((2, m, m), BF16), pltpu.VMEM((2, m, face), BF16)
    table, v0b, *tiles = call(
        functools.partial(table_kernel, fcount, step),
        (
            pltpu.VMEM((NT // KGROUP, NOSC, lanes), BF16),
            doubled,
            tile_shape,
            side,
            side,
        ),
        [SM, SM] + [HB] * 4 + [VM],
        (VM,) * 5,
        [pltpu.SemaphoreType.DMA((3, 2))],
        limit=6,
    )(freq_values, me, tile_h, left_h, right_h, pack_b, v0)

    mask = block_mask[0]
    parity1 = parity.reshape(1)
    image_shape = pltpu.VMEM((m, cols), F32)
    near_rhs = pltpu.VMEM((2 * face, cols), BF16)
    own1, tile, left, right = call(
        functools.partial(own_kernel, True, step),
        (image_shape, tile_shape, side, side),
        [SM, SM] + [HB] * 3 + [VM] * 5,
        (VM,) * 4,
        [near_rhs, pltpu.SemaphoreType.DMA((m // step - 1, 3, 2))],
        limit=10,
        aliases={5: 1, 6: 2, 7: 3},
    )(mask, parity1, tile_h, left_h, right_h, *vmem(*tiles, v0b, near1))
    tile, left, right = vmem(tile, left, right)

    rhs_scratch = pltpu.VMEM((2 * face, cols), BF16)
    pack_a2, pack_b2, token = call(
        faces_kernel,
        (packed, packed, jax.ShapeDtypeStruct((8, 128), F32)),
        [SM, SM, SM, VM, VM, VM, VM],
        (VM, VM, VM),
        [rhs_scratch, pltpu.VMEM((2 * face, 2 * face), BF16)],
        limit=8,
    )(send_a, send_b, parity1, *vmem(own1), left, right, *vmem(far1))
    far2 = far(pack_b2)
    near2 = near(pack_a2)
    v1, v1b = call(
        functools.partial(image_kernel, 512),
        (image_shape, doubled),
        [SM, VM, VM, VM, VM, HB],
        (VM, VM),
        [rhs_scratch],
        limit=8,
    )(parity1, *vmem(own1), left, right, *vmem(far1), token)
    (v1,) = vmem(v1)
    sums1 = call(
        functools.partial(sums_kernel, 128),
        jax.ShapeDtypeStruct((8, half), F32),
        [VM, VM],
        VM,
        limit=4,
    )(v0, v1)

    own2 = call(
        functools.partial(own_kernel, False, step),
        image_shape,
        [SM, SM] + [VM] * 5,
        VM,
        [near_rhs],
        limit=10,
    )(mask, parity1, tile, left, right, *vmem(v1b, near2))

    owner, dof = node_owner[0], node_dof[0]
    number = jnp.arange(nodes_sub, dtype=jnp.int32)
    before = (owner[:, None] == owner[None, :]) & (number[None, :] < number[:, None])
    slot = owner * nodes_own + jnp.sum(before.astype(jnp.int32), axis=1)
    dof_of = jnp.sum(jnp.where(slot[None, :] == number[:, None], dof[None, :], 0), axis=1)
    sums = call(
        functools.partial(second_kernel, 256),
        jax.ShapeDtypeStruct((8, half), F32),
        [SM] + [VM] * 7,
        VM,
        [rhs_scratch],
        limit=8,
    )(parity1, *vmem(own2), left, right, *vmem(far2), v0, v1, sums1)

    picks, bit = [], 1
    while bit < nsub or len(picks) < 2:
        got = exchange(sums, "sub", nsub, bit) if bit < nsub else jnp.zeros_like(sums)
        if bit > 1 and len(picks) < 2:
            rows, sums = call(
                functools.partial(pick_kernel, len(picks) * nodes_sub // 2),
                (
                    pltpu.VMEM((nodes_sub // 2, 2 * cols), F32),
                    jax.ShapeDtypeStruct((8, half), F32),
                ),
                [SM, VM, VM, VM],
                (VM, VM),
                limit=4,
            )(dof_of, v0, v1, sums)
            picks += vmem(rows)
        sums = sums + got
        bit *= 2

    resp, h = call(
        resp_kernel,
        (jax.ShapeDtypeStruct((2, nodes_sub), F32), jax.ShapeDtypeStruct((8, half), F32)),
        [VM, VM, VM, VM],
        (VM, VM),
        limit=4,
    )(sums, motion, *picks)
    arrived = everyone(resp, "freq")
    solution = call(
        sol_kernel,
        jax.ShapeDtypeStruct((m, cols), F32),
        [VM, VM, VM],
        HB,
        [pltpu.VMEM((m, cols), F32), pltpu.SemaphoreType.DMA((6,))],
        limit=6,
    )(h, v0, *vmem(v1))

    spectra = call(
        functools.partial(spec_kernel, 256),
        jax.ShapeDtypeStruct((nodes_own, NOSC), F32),
        [SM, VM, VM],
        HB,
        [
            pltpu.VMEM((lanes, KGROUP * nodes_own), BF16),
            pltpu.VMEM((nodes_own, NOSC), F32),
            pltpu.SemaphoreType.DMA((NOSC // 256,)),
        ],
        limit=8,
    )(me, arrived, *vmem(table))
    return solution[None, None], spectra[None]


def solution(mesh):
    placed = (
        P("sub", "freq", None, None),
        P("sub", "freq", None, None, None),
        P("sub", "freq", None, None, None),
        P("sub", "freq", None, None, None),
        P("sub", None, None),
        P("sub", None),
        P("sub", None),
        P("freq", None),
        P(),
        P("sub", None),
        P("sub", None),
    )
    return jax.shard_map(
        on_device,
        mesh=mesh,
        in_specs=placed,
        out_specs=(P("sub", "freq", None, None), P("sub", "freq", None)),
        check_vma=False,
    )
```
